512 devices in a mesh: grp: 16 (over y_lo, x, core), slab: 32 (over z, y_hi).
Axes of the slice: x: 4, y: 4 (y_hi: 2, y_lo: 2; y = y_hi * 2 + y_lo), z: 16, core: 2. Of those that a mesh axis runs over, the one named last changes fastest.
Arguments:
- amplitudes: float32 [4096, 65536], P('grp', 'slab'), may hold values from -6 to 6, as said below
- ladder_ints: float32 [65536, 1024], P('slab', 'grp'), may hold values from -1 to 1, as said below
- cycle_ints: float32 [16384, 512], P('grp'), may hold values from -1 to 1, as said below
- occ_irrep: int32 [64], replicated, may hold values from 0 to 7, as said below
- vir_irrep: int32 [256], replicated, may hold values from 0 to 7, as said below
Outputs:
- ladder_term: float32 [4096, 1024], P('grp', 'slab')
- cycle_term: float32 [64, 256, 512], P('grp', 'slab')
The draws below stay inside these ranges and needn't reach their ends.
Inputs may be any that keep to these rules, and one draw needn't show every extreme that they name: `occ_irrep`: nondecreasing: the occupied orbitals are ordered by irrep. `vir_irrep`: nondecreasing: the virtual orbitals are ordered by irrep. amplitudes[i * 64 + j, a * 256 + b] is zero unless xor(occ_irrep[i], occ_irrep[j]) equals xor(vir_irrep[a], vir_irrep[b]). ladder_ints[c * 256 + d, a * 256 + b] is zero unless xor(vir_irrep[c], vir_irrep[d]) equals xor(vir_irrep[a], vir_irrep[b]). cycle_ints[k * 256 + c, j * 256 + b] is zero unless xor(occ_irrep[k], vir_irrep[c]) equals xor(occ_irrep[j], vir_irrep[b]).
All inputs are finite; a program needn't handle non-finite values.
Results may differ from the reference program's by a relative error of at most 0.000077.
Values sent between devices are 32-bit elements; how exact they have to be, the bound alone decides.
A program may use at most 64 MiB of HBM per device.

```python
import jax
import jax.numpy as jnp
from jax import lax

NO = 64
NV = 256
AW = 4
JW = 2
PAIRS = 4096
VPAIRS = 65536


def irrep_labels(key, count, salt):
    label_key = jax.random.fold_in(key, salt)
    drawn = jax.random.randint(label_key, (count,), 0, 8)
    positions = jnp.arange(count)
    drawn = jnp.where(positions == 0, 0, jnp.where(positions == 1, 7, drawn))
    return jnp.sort(drawn).astype(jnp.int32)


def pair_irreps(first, second):
    return jnp.bitwise_xor(jnp.repeat(first, second.shape[0]), jnp.tile(second, first.shape[0]))


def draw_occ_irrep(key, part):
    return irrep_labels(key, NO, 11)


def draw_vir_irrep(key, part):
    return irrep_labels(key, NV, 12)


def draw_amplitudes(key, part):
    occ_labels = irrep_labels(key, NO, 11)
    vir_labels = irrep_labels(key, NV, 12)
    key = jax.random.fold_in(key, 3)
    keep = pair_irreps(occ_labels, occ_labels)[:, None] == pair_irreps(vir_labels, vir_labels)[None, :]
    values = jax.random.truncated_normal(key, -6.0, 6.0, (PAIRS, VPAIRS), jnp.float32)
    return jnp.where(keep, values, jnp.float32(0.0))


def draw_ladder_ints(key, part):
    vir_labels = irrep_labels(key, NV, 12)
    key = jax.random.fold_in(key, 5)
    keep = pair_irreps(vir_labels, vir_labels)[:, None] == pair_irreps(vir_labels[:AW], vir_labels)[None, :]
    spread = jnp.sqrt(jnp.float32(8.0) / VPAIRS)
    values = jax.random.truncated_normal(key, -4.0, 4.0, (VPAIRS, AW * NV), jnp.float32)
    return jnp.where(keep, values * spread, jnp.float32(0.0))


def draw_cycle_ints(key, part):
    occ_labels = irrep_labels(key, NO, 11)
    vir_labels = irrep_labels(key, NV, 12)
    key = jax.random.fold_in(key, 7)
    keep = pair_irreps(occ_labels, vir_labels)[:, None] == pair_irreps(occ_labels[:JW], vir_labels)[None, :]
    spread = jnp.sqrt(jnp.float32(8.0) / (NO * NV))
    values = jax.random.truncated_normal(key, -4.0, 4.0, (NO * NV, JW * NV), jnp.float32)
    return jnp.where(keep, values * spread, jnp.float32(0.0))


def setup_inputs(seed: int = 0) -> dict:
    seeds = jax.random.split(jax.random.key(seed), 6)
    amplitudes = draw_amplitudes(jax.random.fold_in(seeds[5], 71), 0)
    ladder_ints = draw_ladder_ints(jax.random.fold_in(seeds[5], 71), 0)
    cycle_ints = draw_cycle_ints(jax.random.fold_in(seeds[5], 71), 0)
    occ_irrep = draw_occ_irrep(jax.random.fold_in(seeds[5], 71), 0)
    vir_irrep = draw_vir_irrep(jax.random.fold_in(seeds[5], 71), 0)
    return dict(amplitudes=amplitudes, ladder_ints=ladder_ints, cycle_ints=cycle_ints, occ_irrep=occ_irrep, vir_irrep=vir_irrep)


def allowed_mask(lab_i, lab_j, lab_a, lab_b):
    left = jnp.bitwise_xor(lab_i, lab_j)
    right = jnp.bitwise_xor(lab_a, lab_b)
    return left == right


def reference(amplitudes, ladder_ints, cycle_ints, occ_irrep, vir_irrep):
    ladder = jnp.dot(amplitudes, ladder_ints, precision=lax.Precision.HIGHEST, preferred_element_type=jnp.float32)
    row_i = jnp.repeat(occ_irrep, NO)
    row_j = jnp.tile(occ_irrep, NO)
    col_a = jnp.repeat(vir_irrep[:AW], NV)
    col_b = jnp.tile(vir_irrep, AW)
    ladder_keep = allowed_mask(row_i[:, None], row_j[:, None], col_a[None, :], col_b[None, :])
    ladder_term = jnp.where(ladder_keep, ladder, jnp.float32(0.0))

    blocks = amplitudes.reshape(NO, NO, NV, NV)
    table = cycle_ints.reshape(NO, NV, JW * NV)

    def one_row(block):
        return jnp.einsum("kac,kcw->aw", block, table, precision=lax.Precision.HIGHEST)

    cycle = lax.map(one_row, blocks)
    col_j = jnp.repeat(occ_irrep[:JW], NV)
    col_jb = jnp.tile(vir_irrep, JW)
    cycle_keep = allowed_mask(occ_irrep[:, None, None], col_j[None, None, :], vir_irrep[None, :, None], col_jb[None, None, :])
    cycle_term = jnp.where(cycle_keep, cycle, jnp.float32(0.0))
    return ladder_term, cycle_term
```

```python
import functools

import jax
import jax.numpy as jnp
from jax import lax
from jax.experimental import pallas as pl
from jax.experimental.pallas import tpu as pltpu
from jax.sharding import PartitionSpec as P

FOLD = 64
IRREPS = 8
MESH = pl.DeviceIdType.MESH
EXACT = lax.Precision.HIGHEST


def allowed_mask(lab_i, lab_j, lab_a, lab_b):
    left = jnp.bitwise_xor(lab_i, lab_j)
    right = jnp.bitwise_xor(lab_a, lab_b)
    return left == right


def dense_path(amplitudes, ladder_ints, cycle_ints, occ_irrep, vir_irrep):
    groups = lax.axis_size("grp")
    slabs = lax.axis_size("slab")
    grp_index = lax.axis_index("grp")
    slab_index = lax.axis_index("slab")
    occ_count = occ_irrep.shape[0]
    vir_count = vir_irrep.shape[0]
    occ_local = amplitudes.shape[0] // occ_count
    vir_local = amplitudes.shape[1] // vir_count
    window = ladder_ints.shape[1] * groups
    ladder_cols = window // slabs
    a_count = window // vir_count
    partial_sum = jnp.dot(
        amplitudes,
        lax.all_gather(ladder_ints, "grp", axis=1, tiled=True),
        precision=lax.Precision.HIGHEST,
        preferred_element_type=jnp.float32,
    )
    ladder = lax.psum_scatter(partial_sum, "slab", scatter_dimension=1, tiled=True)
    occ_mine = lax.dynamic_slice_in_dim(occ_irrep, grp_index * occ_local, occ_local, 0)
    row_i = jnp.repeat(occ_mine, occ_count)
    row_j = jnp.tile(occ_irrep, occ_local)
    col_a = lax.dynamic_slice_in_dim(
        jnp.repeat(vir_irrep[:a_count], vir_count), slab_index * ladder_cols, ladder_cols, 0
    )
    col_b = lax.dynamic_slice_in_dim(
        jnp.tile(vir_irrep, a_count), slab_index * ladder_cols, ladder_cols, 0
    )
    ladder_keep = allowed_mask(row_i[:, None], row_j[:, None], col_a[None, :], col_b[None, :])
    ladder_term = jnp.where(ladder_keep, ladder, jnp.float32(0.0))
    blocks = amplitudes.reshape(occ_local, occ_count, vir_local, vir_count)
    k_local = cycle_ints.shape[0] // vir_count
    cycle_cols = cycle_ints.shape[1]
    cycle_table = cycle_ints.reshape(k_local, vir_count, cycle_cols)
    regrouped = lax.all_to_all(blocks, "grp", split_axis=1, concat_axis=0, tiled=True)
    partial_cycle = jnp.einsum(
        "ikac,kcw->iaw", regrouped, cycle_table, precision=lax.Precision.HIGHEST
    )
    cycle = lax.psum_scatter(partial_cycle, "grp", scatter_dimension=0, tiled=True)
    j_count = cycle_cols // vir_count
    vir_mine = lax.dynamic_slice_in_dim(vir_irrep, slab_index * vir_local, vir_local, 0)
    col_j = jnp.repeat(occ_irrep[:j_count], vir_count)
    col_jb = jnp.tile(vir_irrep, j_count)
    cycle_keep = allowed_mask(
        occ_mine[:, None, None],
        col_j[None, None, :],
        vir_mine[None, :, None],
        col_jb[None, None, :],
    )
    cycle_term = jnp.where(cycle_keep, cycle, jnp.float32(0.0))
    return (ladder_term, cycle_term)


def folded_kernel(
    starts, amp_hbm, lad_hbm, cyc_hbm, lad_out, cyc_out,
    amp, lad, cyc, amp_fold, a2a_send, a2a_recv, cyc_fold, gath, rhs, zed, y_recv, z_send, z_recv, quad,
    lhs, c_part, c_send, c_recv, c_full,
    load_sem, g_ss, g_rs, a_ss, a_rs, y_ss, y_rs, z_ss, z_rs, q_ss, q_rs, c_ss, c_rs,
):
    f32, i32 = jnp.float32, jnp.int32
    g, s = lax.axis_index("grp"), lax.axis_index("slab")
    core, x, y = g % 2, (g // 2) % 4, g // 8
    z, half = s // 2, s % 2

    load_l = pltpu.make_async_copy(lad_hbm, lad, load_sem.at[0])
    load_a = pltpu.make_async_copy(amp_hbm, amp, load_sem.at[1])
    load_w = pltpu.make_async_copy(cyc_hbm, cyc, load_sem.at[2])
    load_l.start()
    load_a.start()
    load_w.start()

    barrier = pltpu.get_barrier_semaphore()

    @pl.loop(1, 16)
    def _(r):
        pl.semaphore_signal(barrier, inc=1, device_id=((g + r) % 16, s), device_id_type=MESH)
        pl.semaphore_signal(barrier, inc=1, device_id=(g, ((z + r) % 16) * 2 + half), device_id_type=MESH)

    pl.semaphore_signal(barrier, inc=1, device_id=(g, z * 2 + (1 - half)), device_id_type=MESH)

    def iota(shape, dim):
        return lax.broadcasted_iota(i32, shape, dim)

    def label(index, base):
        total = jnp.where(index >= starts[base + 1], 1, 0)
        for v in range(2, IRREPS):
            total = total + jnp.where(index >= starts[base + v], 1, 0)
        return total

    occ_label = functools.partial(label, base=0)
    vir_label = functools.partial(label, base=IRREPS)
    low64 = iota((1, 128), 1) < 64

    def pack_pair(first, second):
        keep = jnp.where(low64, first, second)
        move = jnp.where(low64, second, first)
        return keep + pltpu.roll(move, 64, 1)

    def swap_pair(first, second):
        return (
            jnp.where(low64, first, pltpu.roll(second, 64, 1)),
            jnp.where(low64, pltpu.roll(first, 64, 1), second),
        )

    def regroup(src, dst, blocks):
        low4 = iota((8, 1), 0) < 4

        @pl.loop(0, 8)
        def _(q):
            for n in range(0, blocks, 2):
                for c in range(src.shape[1] // 128):
                    cols = slice(128 * c, 128 * c + 128)
                    one = src[pl.ds(pl.multiple_of(64 * n + 8 * q, 8), 8), cols]
                    two = src[pl.ds(pl.multiple_of(64 * n + 64 + 8 * q, 8), 8), cols]
                    dst[2 * q, c, 4 * n : 4 * n + 8, :] = jnp.where(low4, one, pltpu.roll(two, 4, 0))
                    dst[2 * q + 1, c, 4 * n : 4 * n + 8, :] = jnp.where(low4, pltpu.roll(one, 4, 0), two)

    load_l.wait()

    @pl.loop(0, 4)
    def _(c):
        parts = []
        for c_half in range(2):
            base = 256 * c + 1024 * c_half
            part = lad[pl.ds(pl.multiple_of(base, 64), 64), :]
            for m in range(1, 4):
                part = part + lad[pl.ds(pl.multiple_of(base + 64 * m, 64), 64), :]
            parts.append(part)
        gath[g, pl.ds(pl.multiple_of(64 * c, 64), 64), :] = jnp.concatenate(parts, axis=1)

    pl.semaphore_wait(barrier, 31)

    def at(y_, x_, core_):
        return (y_ * 4 + x_ % 4) * 2 + core_

    sib, y_dev = at(y, x, 1 - core), at(1 - y, x, core)
    right, left = at(y, x + 1, core), at(y, x + 3, core)
    y_right, y_left = at(1 - y, x + 1, core), at(1 - y, x + 3, core)
    across, y_across = at(y, x + 2, core), at(1 - y, x + 2, core)

    def g_copy(k, slot, dev, rows=slice(None)):
        ref = gath.at[slot] if rows == slice(None) else gath.at[slot, rows]
        return pltpu.make_async_remote_copy(
            src_ref=ref, dst_ref=ref, send_sem=g_ss.at[k], recv_sem=g_rs.at[k],
            device_id=(dev, s), device_id_type=MESH,
        )

    lower, upper = pl.ds(0, 128), pl.ds(128, 128)
    moves = [
        g_copy(0, g, y_dev), g_copy(1, g, right), g_copy(2, g, left), g_copy(3, g, sib),
        g_copy(4, y_dev, right), g_copy(5, y_dev, left), g_copy(6, y_dev, sib),
        g_copy(7, left, right, lower), g_copy(8, right, left, upper),
        g_copy(9, y_left, right, lower), g_copy(10, y_right, left, upper),
        g_copy(11, left, sib), g_copy(12, right, sib), g_copy(13, y_left, sib), g_copy(14, y_right, sib),
        g_copy(15, across, sib), g_copy(16, y_across, sib),
    ]
    for k in range(4):
        moves[k].start()

    load_a.wait()

    @pl.loop(0, 16)
    def _(r):
        rows = pl.ds(pl.multiple_of(16 * r, 16), 16)
        for m in range(4):
            even = amp[rows, 512 * m : 512 * m + 128] + amp[rows, 512 * m + 128 : 512 * m + 256]
            odd = amp[rows, 512 * m + 256 : 512 * m + 384] + amp[rows, 512 * m + 384 : 512 * m + 512]
            amp_fold[rows, 128 * m : 128 * m + 128] = pack_pair(even, odd)

    regroup(amp_fold, a2a_send, 4)
    moves[0].wait_recv()
    for k in range(4, 7):
        moves[k].start()

    def a_copy(r):
        to = (g + r) % 16
        return pltpu.make_async_remote_copy(
            src_ref=a2a_send.at[to], dst_ref=a2a_recv.at[:, pl.ds(pl.multiple_of(16 * g, 16), 16)],
            send_sem=a_ss.at[r], recv_sem=a_rs.at[r], device_id=(to, s), device_id_type=MESH,
        )

    a2a_recv[:, pl.ds(pl.multiple_of(16 * g, 16), 16), :] = a2a_send[g]

    @pl.loop(1, 16)
    def _(r):
        a_copy(r).start()

    moves[1].wait_recv()
    moves[7].start()
    moves[11].start()
    moves[2].wait_recv()
    moves[8].start()
    moves[12].start()

    load_w.wait()

    @pl.loop(0, 4)
    def _(k):
        part = cyc[pl.ds(pl.multiple_of(256 * k, 64), 64), :]
        for m in range(1, 4):
            part = part + cyc[pl.ds(pl.multiple_of(256 * k + 64 * m, 64), 64), :]
        cyc_fold[pl.ds(pl.multiple_of(64 * k, 64), 64), :] = part

    moves[4].wait_recv()
    moves[9].start()
    moves[13].start()
    moves[5].wait_recv()
    moves[10].start()
    moves[14].start()
    moves[7].wait_recv()
    moves[8].wait_recv()
    moves[15].start()
    moves[9].wait_recv()
    moves[10].wait_recv()
    moves[16].start()
    for k in (3, 6, 11, 12, 13, 14, 15, 16):
        moves[k].wait_recv()

    lane = iota((1, 128), 1)
    lane_block = lane // 32

    def pair_label(i):
        return occ_label(4 * g + i) ^ occ_label(iota((64, 128), 0))

    row_label = jnp.concatenate([pair_label(i) for i in range(4)], axis=0)

    @pl.loop(0, 4)
    def _(a):
        for pair in range(2):
            low, high = swap_pair(gath[4 * a + 2 * pair], gath[4 * a + 2 * pair + 1])
            rhs[0:256, 128 * pair : 128 * pair + 128] = low
            rhs[256:512, 128 * pair : 128 * pair + 128] = high
        product = jnp.dot(amp_fold[...], rhs[...], precision=EXACT, preferred_element_type=f32)
        kept = [
            jnp.where(
                row_label == (vir_label(a) ^ vir_label(lane + 128 * part)),
                product[:, 128 * part : 128 * part + 128], f32(0.0),
            )
            for part in range(2)
        ]
        once = kept[0] + kept[1]
        once = once + pltpu.roll(once, 64, 1)
        turned = pltpu.roll(once, 32, 1)
        o = [once[64 * i : 64 * i + 64] for i in range(4)]
        t = [turned[64 * i : 64 * i + 64] for i in range(4)]
        rows = pl.ds(pl.multiple_of(64 * a, 64), 64)

        def merge(p0, p1, p2, p3):
            return jnp.where(
                lane_block < 2, jnp.where(lane_block == 0, p0, p1), jnp.where(lane_block == 2, p2, p3)
            )

        zed[0, rows, :] = merge(o[0], t[1], o[2], t[3])
        zed[1, rows, :] = merge(t[0], o[1], t[2], o[3])

    y_copy = pltpu.make_async_remote_copy(
        src_ref=zed.at[1 - half], dst_ref=y_recv, send_sem=y_ss, recv_sem=y_rs,
        device_id=(g, z * 2 + (1 - half)), device_id_type=MESH,
    )
    y_copy.start()

    @pl.loop(1, 16)
    def _(r):
        a_copy(r).wait_recv()

    for m in range(4):
        piece = [a2a_recv[m, pl.ds(k, 64, stride=4), :] for k in range(4)]
        for p in range(2):
            even, odd = swap_pair(piece[2 * p], piece[2 * p + 1])
            lhs[128 * m : 128 * m + 64, 128 * p : 128 * p + 128] = even
            lhs[128 * m + 64 : 128 * m + 128, 128 * p : 128 * p + 128] = odd

    @pl.loop(0, 2)
    def _(h):
        rows = pl.ds(pl.multiple_of(256 * h, 256), 256)
        r_id = iota((256, 128), 0)
        ia_label = occ_label(r_id % 64) ^ vir_label(8 * s + 4 * h + r_id // 64)
        folds = []
        for j in range(2):
            product = jnp.dot(
                lhs[rows, :], cyc_fold[:, 256 * j : 256 * j + 256], precision=EXACT, preferred_element_type=f32
            )
            kept = [
                jnp.where(
                    ia_label == (occ_label(jnp.int32(j)) ^ vir_label(lane + 128 * part)),
                    product[:, 128 * part : 128 * part + 128], f32(0.0),
                )
                for part in range(2)
            ]
            folds.append(kept[0] + kept[1])
        c_part[rows, :] = pack_pair(folds[0], folds[1])

    regroup(c_part, c_send, 8)

    def c_copy(r):
        to = (g + r) % 16
        return pltpu.make_async_remote_copy(
            src_ref=c_send.at[to, 0], dst_ref=c_recv.at[g],
            send_sem=c_ss.at[r], recv_sem=c_rs.at[r], device_id=(to, s), device_id_type=MESH,
        )

    @pl.loop(1, 16)
    def _(r):
        c_copy(r).start()

    c_recv[g] = c_send[g, 0]

    y_copy.wait_recv()
    z_send[...] = zed[half] + y_recv[...]

    def z_copy(r):
        to = (z + r) % 16
        return pltpu.make_async_remote_copy(
            src_ref=z_send.at[pl.ds(pl.multiple_of(16 * to, 16), 16)], dst_ref=z_recv.at[z],
            send_sem=z_ss.at[r], recv_sem=z_rs.at[r], device_id=(g, to * 2 + half), device_id_type=MESH,
        )

    @pl.loop(1, 16)
    def _(r):
        z_copy(r).start()

    z_recv[z] = z_send[pl.ds(pl.multiple_of(16 * z, 16), 16), :]

    @pl.loop(1, 16)
    def _(r):
        c_copy(r).wait_recv()

    total = c_recv[0]
    for n in range(1, 16):
        total = total + c_recv[n]
    turned = pltpu.roll(total, 64, 1)
    both = [jnp.where(low64, total, turned), jnp.where(low64, turned, total)]
    r_id = iota((32, 128), 0)
    ia_label = occ_label(4 * g + r_id % 4) ^ vir_label(8 * s + r_id // 4)
    for part in range(4):
        j, b0 = part // 2, 128 * (part % 2)
        c_full[part] = jnp.where(
            ia_label == (occ_label(jnp.int32(j)) ^ vir_label(lane + b0)), both[j], f32(0.0)
        )
    for i in range(4):
        for part in range(4):
            cols = slice(128 * part, 128 * part + 128)
            cyc_out[i, :, cols] = c_full[part, pl.ds(i, 8, stride=4), :]

    @pl.loop(1, 16)
    def _(r):
        z_copy(r).wait_recv()

    total = z_recv[0]
    for n in range(1, 16):
        total = total + z_recv[n]
    mine = pl.ds(pl.multiple_of(16 * (z % 4), 16), 16)
    quad[mine, :] = total

    def q_copy(d):
        to = 4 * (z // 4) + (z + d) % 4
        return pltpu.make_async_remote_copy(
            src_ref=quad.at[mine], dst_ref=quad.at[mine],
            send_sem=q_ss.at[d], recv_sem=q_rs.at[d], device_id=(g, to * 2 + half), device_id_type=MESH,
        )

    for d in range(1, 4):
        q_copy(d).start()
    for d in range(1, 4):
        q_copy(d).wait_recv()

    col = vir_label(z // 4) ^ vir_label(32 * (s % 8) + lane)
    full = quad[...]
    for i in range(4):
        here = full if i == 0 else pltpu.roll(full, 128 - 32 * i, 1)
        kept = jnp.where(pair_label(i) == col, here, f32(0.0))
        lad_out[64 * i : 64 * i + 64, :] = kept[:, 0:32]

    for move in moves:
        move.wait_send()
    y_copy.wait_send()
    for d in range(1, 4):
        q_copy(d).wait_send()

    @pl.loop(1, 16)
    def _(r):
        a_copy(r).wait_send()
        c_copy(r).wait_send()
        z_copy(r).wait_send()


def folded_path(starts, amplitudes, ladder_ints, cycle_ints):
    f32 = jnp.float32
    vmem = pltpu.VMEM
    dma = pltpu.SemaphoreType.DMA
    return pl.pallas_call(
        folded_kernel,
        out_shape=(
            jax.ShapeDtypeStruct((256, 32), f32),
            jax.ShapeDtypeStruct((4, 8, 512), f32),
        ),
        in_specs=[pl.BlockSpec(memory_space=pltpu.SMEM)] + [pl.BlockSpec(memory_space=pl.ANY)] * 3,
        out_specs=[pl.BlockSpec(memory_space=pltpu.VMEM)] * 2,
        scratch_shapes=[
            vmem((256, 2048), f32), vmem((2048, 64), f32), vmem((1024, 512), f32),
            vmem((256, 512), f32), vmem((16, 4, 16, 128), f32), vmem((4, 256, 128), f32), vmem((256, 512), f32),
            vmem((16, 256, 128), f32), vmem((512, 256), f32), vmem((2, 256, 128), f32), vmem((256, 128), f32),
            vmem((256, 128), f32), vmem((16, 16, 128), f32), vmem((64, 128), f32),
            vmem((512, 256), f32), vmem((512, 128), f32), vmem((16, 1, 32, 128), f32), vmem((16, 32, 128), f32),
            vmem((4, 32, 128), f32),
            dma((3,)), dma((17,)), dma((17,)), dma((16,)), dma((16,)), dma, dma,
            dma((16,)), dma((16,)), dma((4,)), dma((4,)), dma((16,)), dma((16,)),
        ],
        compiler_params=pltpu.CompilerParams(
            collective_id=0, has_side_effects=True, vmem_limit_bytes=40 * 1024 * 1024
        ),
        cost_estimate=pl.CostEstimate(flops=400_000_000, bytes_accessed=5_000_000, transcendentals=0),
    )(starts, amplitudes, ladder_ints, cycle_ints)


def per_device(amplitudes, ladder_ints, cycle_ints, occ_irrep, vir_irrep):
    irreps = jnp.arange(IRREPS, dtype=jnp.int32)[:, None]
    occ_starts = jnp.sum((occ_irrep[None, :] < irreps).astype(jnp.int32), axis=1)
    vir_starts = jnp.sum((vir_irrep[None, :] < irreps).astype(jnp.int32), axis=1)
    runs = jnp.sum((vir_irrep[None, :] == irreps).astype(jnp.int32), axis=1)
    starts = jnp.concatenate([occ_starts, vir_starts])
    return lax.cond(
        jnp.max(runs) <= FOLD,
        lambda: tuple(folded_path(starts, amplitudes, ladder_ints, cycle_ints)),
        lambda: dense_path(amplitudes, ladder_ints, cycle_ints, occ_irrep, vir_irrep),
    )


def solution(mesh):
    return jax.shard_map(
        per_device,
        mesh=mesh,
        in_specs=(P("grp", "slab"), P("slab", "grp"), P("grp", None), P(), P()),
        out_specs=(P("grp", "slab"), P("grp", "slab", None)),
        check_vma=False,
    )
```

```python
import functools

import jax
import jax.numpy as jnp
from jax import lax
from jax.experimental import pallas as pl
from jax.experimental.pallas import tpu as pltpu
from jax.sharding import PartitionSpec as P

FOLD = 64
IRREPS = 8
MESH = pl.DeviceIdType.MESH


def allowed_mask(lab_i, lab_j, lab_a, lab_b):
    left = jnp.bitwise_xor(lab_i, lab_j)
    right = jnp.bitwise_xor(lab_a, lab_b)
    return left == right


def gather_cols(block):
    groups = lax.axis_size("grp")
    copies = jnp.broadcast_to(block[None], (groups,) + block.shape)
    parts = lax.all_to_all(copies, "grp", split_axis=0, concat_axis=0, tiled=True)
    return jnp.moveaxis(parts, 0, 1).reshape(block.shape[0], groups * block.shape[1])


def sum_parts(partial, axis, dim):
    count = lax.axis_size(axis)
    shape = partial.shape
    split = partial.reshape(shape[:dim] + (count, shape[dim] // count) + shape[dim + 1 :])
    parts = lax.all_to_all(split, axis, split_axis=dim, concat_axis=dim, tiled=True)
    return jnp.sum(parts, axis=dim)


def dense_path(amplitudes, ladder_ints, cycle_ints, occ_irrep, vir_irrep):
    groups = lax.axis_size("grp")
    slabs = lax.axis_size("slab")
    grp_index = lax.axis_index("grp")
    slab_index = lax.axis_index("slab")
    occ_count = occ_irrep.shape[0]
    vir_count = vir_irrep.shape[0]
    occ_local = amplitudes.shape[0] // occ_count
    vir_local = amplitudes.shape[1] // vir_count
    window = ladder_ints.shape[1] * groups
    ladder_cols = window // slabs
    a_count = window // vir_count
    partial_sum = jnp.dot(
        amplitudes,
        gather_cols(ladder_ints),
        precision=lax.Precision.HIGHEST,
        preferred_element_type=jnp.float32,
    )
    ladder = sum_parts(partial_sum, "slab", 1)
    occ_mine = lax.dynamic_slice_in_dim(occ_irrep, grp_index * occ_local, occ_local, 0)
    row_i = jnp.repeat(occ_mine, occ_count)
    row_j = jnp.tile(occ_irrep, occ_local)
    col_a = lax.dynamic_slice_in_dim(
        jnp.repeat(vir_irrep[:a_count], vir_count), slab_index * ladder_cols, ladder_cols, 0
    )
    col_b = lax.dynamic_slice_in_dim(
        jnp.tile(vir_irrep, a_count), slab_index * ladder_cols, ladder_cols, 0
    )
    ladder_keep = allowed_mask(row_i[:, None], row_j[:, None], col_a[None, :], col_b[None, :])
    ladder_term = jnp.where(ladder_keep, ladder, jnp.float32(0.0))
    blocks = amplitudes.reshape(occ_local, occ_count, vir_local, vir_count)
    k_local = cycle_ints.shape[0] // vir_count
    cycle_cols = cycle_ints.shape[1]
    cycle_table = cycle_ints.reshape(k_local, vir_count, cycle_cols)
    regrouped = lax.all_to_all(blocks, "grp", split_axis=1, concat_axis=0, tiled=True)
    partial_cycle = jnp.einsum(
        "ikac,kcw->iaw", regrouped, cycle_table, precision=lax.Precision.HIGHEST
    )
    cycle = sum_parts(partial_cycle, "grp", 0)
    j_count = cycle_cols // vir_count
    vir_mine = lax.dynamic_slice_in_dim(vir_irrep, slab_index * vir_local, vir_local, 0)
    col_j = jnp.repeat(occ_irrep[:j_count], vir_count)
    col_jb = jnp.tile(vir_irrep, j_count)
    cycle_keep = allowed_mask(
        occ_mine[:, None, None],
        col_j[None, None, :],
        vir_mine[None, :, None],
        col_jb[None, None, :],
    )
    cycle_term = jnp.where(cycle_keep, cycle, jnp.float32(0.0))
    return (ladder_term, cycle_term)


def folded_kernel(
    occ_hbm, vir_hbm, amp_hbm, lad_hbm, cyc_hbm, lad_out, cyc_out,
    occ_v, vir_v, amp, lad, cyc, amp_fold, amp_hi, amp_lo, a2a_send, a2a_recv, cyc_hi, cyc_lo, gath,
    zed, y_recv, z_send, z_recv, quad, lhs_hi, lhs_lo, c_part, c_send, c_recv, c_full,
    load_sem, g_ss, g_rs, a_ss, a_rs, y_ss, y_rs, z_ss, z_rs, q_ss, q_rs, c_ss, c_rs,
):
    f32, i32, bf16 = jnp.float32, jnp.int32, jnp.bfloat16
    g, s = lax.axis_index("grp"), lax.axis_index("slab")
    core, x, y = g % 2, (g // 2) % 4, g // 8
    z, half = s // 2, s % 2

    load_l = pltpu.make_async_copy(lad_hbm, lad, load_sem.at[0])
    load_a = pltpu.make_async_copy(amp_hbm, amp, load_sem.at[1])
    load_w = pltpu.make_async_copy(cyc_hbm, cyc, load_sem.at[2])
    load_o = pltpu.make_async_copy(occ_hbm, occ_v, load_sem.at[3])
    load_v = pltpu.make_async_copy(vir_hbm, vir_v, load_sem.at[4])
    load_l.start()
    load_o.start()
    load_v.start()
    load_a.start()
    load_w.start()

    barrier = pltpu.get_barrier_semaphore()

    @pl.loop(1, 16)
    def _(r):
        pl.semaphore_signal(barrier, inc=1, device_id=((g + r) % 16, s), device_id_type=MESH)
        pl.semaphore_signal(barrier, inc=1, device_id=(g, ((z + r) % 16) * 2 + half), device_id_type=MESH)

    pl.semaphore_signal(barrier, inc=1, device_id=(g, z * 2 + (1 - half)), device_id_type=MESH)

    def iota(shape, dim):
        return lax.broadcasted_iota(i32, shape, dim)

    def split(value):
        high = value.astype(bf16)
        return high, (value - high.astype(f32)).astype(bf16)

    low64 = iota((1, 128), 1) < 64
    lane = iota((1, 128), 1)

    def pack_pair(first, second):
        keep = jnp.where(low64, first, second)
        move = jnp.where(low64, second, first)
        return keep + pltpu.roll(move, 64, 1)

    def swap_pair(first, second):
        return (
            jnp.where(low64, first, pltpu.roll(second, 64, 1)),
            jnp.where(low64, pltpu.roll(first, 64, 1), second),
        )

    def fold_pair(src, rows, m):
        at = [src[rows, 512 * m + 128 * n : 512 * m + 128 * n + 128] for n in range(4)]
        return pack_pair(at[0] + at[1], at[2] + at[3])

    def regroup(src, dst, blocks):
        low4 = iota((8, 1), 0) < 4

        @pl.loop(0, 8)
        def _(q):
            for n in range(0, blocks, 2):
                for c in range(src.shape[1] // 128):
                    cols = slice(128 * c, 128 * c + 128)
                    one = src[pl.ds(pl.multiple_of(64 * n + 8 * q, 8), 8), cols]
                    two = src[pl.ds(pl.multiple_of(64 * n + 64 + 8 * q, 8), 8), cols]
                    dst[2 * q, c, 4 * n : 4 * n + 8, :] = jnp.where(low4, one, pltpu.roll(two, 4, 0))
                    dst[2 * q + 1, c, 4 * n : 4 * n + 8, :] = jnp.where(low4, pltpu.roll(one, 4, 0), two)

    load_l.wait()
    for m in range(4):
        gath[g, :, 128 * m : 128 * m + 128] = fold_pair(lad, slice(0, 64), m)

    pl.semaphore_wait(barrier, 31)

    def dev(y_, x_, core_):
        return (y_ * 4 + x_ % 4) * 2 + core_

    turn = 1 - 2 * (x % 2)
    sib, y_dev = dev(y, x, 1 - core), dev(1 - y, x, core)
    mate, other = dev(y, x + 4 + turn, core), dev(y, x + 4 - turn, core)
    y_mate, y_other = dev(1 - y, x + 4 + turn, core), dev(1 - y, x + 4 - turn, core)
    across, y_across = dev(y, x + 2, core), dev(1 - y, x + 2, core)

    def g_copy(k, slot, to, rows=None):
        ref = gath.at[slot] if rows is None else gath.at[slot, rows]
        return pltpu.make_async_remote_copy(
            src_ref=ref, dst_ref=ref, send_sem=g_ss.at[k], recv_sem=g_rs.at[k],
            device_id=(to, s), device_id_type=MESH,
        )

    lower, upper = pl.ds(0, 32), pl.ds(32, 32)
    moves = [
        g_copy(0, g, y_dev), g_copy(1, g, mate), g_copy(2, g, other), g_copy(3, g, sib),
        g_copy(4, y_dev, mate), g_copy(5, y_dev, other), g_copy(6, y_dev, sib),
        g_copy(7, mate, other, lower), g_copy(8, other, mate, upper),
        g_copy(9, y_mate, other, lower), g_copy(10, y_other, mate, upper),
        g_copy(11, mate, sib), g_copy(12, other, sib), g_copy(13, y_mate, sib), g_copy(14, y_other, sib),
        g_copy(15, across, sib), g_copy(16, y_across, sib),
    ]

    def go(*numbers):
        for k in numbers:
            moves[k].start()

    def got(*numbers):
        for k in numbers:
            moves[k].wait_recv()

    go(0, 1, 2, 3)

    load_a.wait()

    @pl.loop(0, 16)
    def _(r):
        rows = pl.ds(pl.multiple_of(16 * r, 16), 16)
        for m in range(4):
            cols = slice(128 * m, 128 * m + 128)
            folded = fold_pair(amp, rows, m)
            amp_fold[rows, cols] = folded
            amp_hi[rows, cols], amp_lo[rows, cols] = split(folded)

    regroup(amp_fold, a2a_send, 4)
    got(0)
    go(4, 5, 6)
    got(1)
    go(7, 11)
    got(2)
    go(8, 12)

    mine16 = pl.ds(pl.multiple_of(16 * g, 16), 16)

    def a_copy(r):
        to = (g + r) % 16
        return pltpu.make_async_remote_copy(
            src_ref=a2a_send.at[to], dst_ref=a2a_recv.at[:, mine16],
            send_sem=a_ss.at[r], recv_sem=a_rs.at[r], device_id=(to, s), device_id_type=MESH,
        )

    @pl.loop(1, 16)
    def _(r):
        a_copy(r).start()

    a2a_recv[:, mine16, :] = a2a_send[g]

    load_o.wait()
    load_v.wait()

    def run_starts(ref):
        return [
            jnp.sum(jnp.where(ref[...] < v, 1.0, 0.0), axis=1, keepdims=True).astype(i32) for v in range(1, IRREPS)
        ]

    occ_starts, vir_starts = run_starts(occ_v), run_starts(vir_v)

    def label(index, starts):
        total = jnp.where(index >= starts[0], 1, 0)
        for start in starts[1:]:
            total = total + jnp.where(index >= start, 1, 0)
        return total

    def occ_label(index):
        return label(index, occ_starts)

    def vir_label(index):
        return label(index, vir_starts)

    zero = jnp.zeros((1, 128), i32)

    def pair_label(part):
        return occ_label(4 * g + 2 * part + lane // 64) ^ occ_label(lane % 64)

    ij_label = [pair_label(part) for part in range(2)]
    row_label = [vir_label(iota((64, 128), 0) + 64 * m) for m in range(4)]

    def dot(first, second, dims):
        return lax.dot_general(first, second, (dims, ((), ())), preferred_element_type=f32)

    def dot3(a_hi, a_lo, b_hi, b_lo, dims):
        return dot(a_hi, b_hi, dims) + (dot(a_hi, b_lo, dims) + dot(a_lo, b_hi, dims))

    order = [2 * y + x // 2, 2 * (1 - y) + x // 2, 2 * y + 1 - x // 2, 2 * (1 - y) + 1 - x // 2]

    def y_copy(n):
        return pltpu.make_async_remote_copy(
            src_ref=zed.at[1 - half, order[n]], dst_ref=y_recv.at[order[n]],
            send_sem=y_ss.at[n], recv_sem=y_rs.at[n],
            device_id=(g, z * 2 + (1 - half)), device_id_type=MESH,
        )

    def z_copy(to):
        r = (to - z + 16) % 16
        return pltpu.make_async_remote_copy(
            src_ref=z_send.at[to], dst_ref=z_recv.at[z],
            send_sem=z_ss.at[r], recv_sem=z_rs.at[r], device_id=(g, to * 2 + half), device_id_type=MESH,
        )

    def ladder_product(n):
        a = order[n]
        hi, lo = split(gath[pl.ds(4 * a, 4)].reshape(256, 512))
        product = dot3(hi, lo, amp_hi[...], amp_lo[...], ((1,), (1,)))
        a_label = vir_label(zero + a)
        for part in range(2):
            cols = slice(128 * part, 128 * part + 128)
            want = ij_label[part] ^ a_label
            total = jnp.where(row_label[0] == want, product[0:64, cols], f32(0.0))
            for m in range(1, 4):
                total = total + jnp.where(row_label[m] == want, product[64 * m : 64 * m + 64, cols], f32(0.0))
            zed[0, a, :, cols] = total[0:32]
            zed[1, a, :, cols] = total[32:64]
        y_copy(n).start()

    def ladder_sums(n):
        a = order[n]
        y_copy(n).wait_recv()
        total = zed[half, a] + y_recv[a]
        for q in range(4):
            z_send[4 * a + q] = total[8 * q : 8 * q + 8]
            to = 4 * a + q

            @pl.when(to != z)
            def _():
                z_copy(to).start()

    got(3, 11)
    ladder_product(0)
    got(4)
    go(9, 13)
    got(5)
    go(10, 14)

    load_w.wait()

    @pl.loop(0, 4)
    def _(k):
        part = cyc[pl.ds(pl.multiple_of(256 * k, 64), 64), :]
        for m in range(1, 4):
            part = part + cyc[pl.ds(pl.multiple_of(256 * k + 64 * m, 64), 64), :]
        rows = pl.ds(pl.multiple_of(64 * k, 64), 64)
        cyc_hi[rows, :], cyc_lo[rows, :] = split(part)

    got(7, 8)
    go(15)
    got(6, 13)
    ladder_product(1)
    ladder_sums(0)
    got(9, 10)
    go(16)
    got(12, 15)
    ladder_product(2)
    ladder_sums(1)
    got(14, 16)
    ladder_product(3)
    ladder_sums(2)

    @pl.loop(1, 16)
    def _(r):
        a_copy(r).wait_recv()

    for m in range(4):
        piece = [a2a_recv[m, pl.ds(k, 64, stride=4), :] for k in range(4)]
        for p in range(2):
            even, odd = swap_pair(piece[2 * p], piece[2 * p + 1])
            cols = slice(128 * p, 128 * p + 128)
            for at, value in ((128 * m, even), (128 * m + 64, odd)):
                lhs_hi[at : at + 64, cols], lhs_lo[at : at + 64, cols] = split(value)

    ladder_sums(3)
    z_recv[z] = z_send[z]

    jb_label = [
        occ_label(zero + part // 2) ^ vir_label(lane + 128 * (part % 2)) for part in range(4)
    ]

    @pl.loop(0, 2)
    def _(h):
        rows = pl.ds(pl.multiple_of(256 * h, 256), 256)
        r_id = iota((256, 128), 0)
        ia_label = occ_label(r_id % 64) ^ vir_label(8 * s + 4 * h + r_id // 64)
        folds = []
        for j in range(2):
            cols = slice(256 * j, 256 * j + 256)
            product = dot3(lhs_hi[rows, :], lhs_lo[rows, :], cyc_hi[:, cols], cyc_lo[:, cols], ((1,), (0,)))
            kept = [
                jnp.where(ia_label == jb_label[2 * j + part], product[:, 128 * part : 128 * part + 128], f32(0.0))
                for part in range(2)
            ]
            folds.append(kept[0] + kept[1])
        c_part[rows, :] = pack_pair(folds[0], folds[1])

    regroup(c_part, c_send, 8)

    def c_copy(r):
        to = (g + r) % 16
        return pltpu.make_async_remote_copy(
            src_ref=c_send.at[to, 0], dst_ref=c_recv.at[g],
            send_sem=c_ss.at[r], recv_sem=c_rs.at[r], device_id=(to, s), device_id_type=MESH,
        )

    @pl.loop(1, 16)
    def _(r):
        c_copy(r).start()

    c_recv[g] = c_send[g, 0]

    def z_arrival(r):
        return pltpu.make_async_remote_copy(
            src_ref=z_send.at[z], dst_ref=z_recv.at[z], send_sem=z_ss.at[r], recv_sem=z_rs.at[r],
            device_id=(g, ((z + r) % 16) * 2 + half), device_id_type=MESH,
        )

    @pl.loop(1, 16)
    def _(r):
        z_arrival(r).wait_recv()

    total = z_recv[0]
    for n in range(1, 16):
        total = total + z_recv[n]
    quarter = z % 4
    quad[quarter] = total

    def q_copy(d):
        to = 4 * (z // 4) + (z + d) % 4
        return pltpu.make_async_remote_copy(
            src_ref=quad.at[quarter], dst_ref=quad.at[quarter],
            send_sem=q_ss.at[d], recv_sem=q_rs.at[d], device_id=(g, to * 2 + half), device_id_type=MESH,
        )

    for d in range(1, 4):
        q_copy(d).start()

    @pl.loop(1, 16)
    def _(r):
        c_copy(r).wait_recv()

    total = c_recv[0]
    for n in range(1, 16):
        total = total + c_recv[n]
    turned = pltpu.roll(total, 64, 1)
    both = [jnp.where(low64, total, turned), jnp.where(low64, turned, total)]
    r_id = iota((32, 128), 0)
    ia_label = occ_label(4 * g + r_id % 4) ^ vir_label(8 * s + r_id // 4)
    for part in range(4):
        c_full[part] = jnp.where(ia_label == jb_label[part], both[part // 2], f32(0.0))
    for i in range(4):
        for part in range(4):
            cyc_out[i, :, 128 * part : 128 * part + 128] = c_full[part, pl.ds(i, 8, stride=4), :]

    for d in range(1, 4):
        q_copy(d).wait_recv()

    b_label = vir_label(zero + z // 4) ^ vir_label(32 * (s % 8) + iota((32, 128), 0))
    full = quad[...].reshape(32, 256)
    for part in range(2):
        cols = slice(128 * part, 128 * part + 128)
        lad_out[:, cols] = jnp.where(ij_label[part] == b_label, full[:, cols], f32(0.0))

    for move in moves:
        move.wait_send()
    for d in range(1, 4):
        q_copy(d).wait_send()

    for n in range(4):
        y_copy(n).wait_send()

    @pl.loop(1, 16)
    def _(r):
        a_copy(r).wait_send()
        c_copy(r).wait_send()
        z_arrival(r).wait_send()


def folded_path(amplitudes, ladder_ints, cycle_ints, occ_irrep, vir_irrep):
    f32, bf16 = jnp.float32, jnp.bfloat16
    vmem = pltpu.VMEM
    dma = pltpu.SemaphoreType.DMA
    ladder, cycle = pl.pallas_call(
        folded_kernel,
        out_shape=(
            jax.ShapeDtypeStruct((32, 256), f32),
            jax.ShapeDtypeStruct((4, 8, 512), f32),
        ),
        in_specs=[pl.BlockSpec(memory_space=pl.ANY)] * 5,
        out_specs=[pl.BlockSpec(memory_space=pltpu.VMEM)] * 2,
        scratch_shapes=[
            vmem((1, 64), jnp.int32), vmem((1, 256), jnp.int32),
            vmem((256, 2048), f32), vmem((64, 2048), f32), vmem((1024, 512), f32),
            vmem((256, 512), f32), vmem((256, 512), bf16), vmem((256, 512), bf16),
            vmem((16, 4, 16, 128), f32), vmem((4, 256, 128), f32),
            vmem((256, 512), bf16), vmem((256, 512), bf16), vmem((16, 64, 512), f32),
            vmem((2, 4, 32, 256), f32), vmem((4, 32, 256), f32), vmem((16, 8, 256), f32), vmem((16, 8, 256), f32),
            vmem((4, 8, 256), f32), vmem((512, 256), bf16), vmem((512, 256), bf16),
            vmem((512, 128), f32), vmem((16, 1, 32, 128), f32), vmem((16, 32, 128), f32), vmem((4, 32, 128), f32),
            dma((5,)), dma((17,)), dma((17,)), dma((16,)), dma((16,)), dma((4,)), dma((4,)),
            dma((16,)), dma((16,)), dma((4,)), dma((4,)), dma((16,)), dma((16,)),
        ],
        compiler_params=pltpu.CompilerParams(
            collective_id=0, has_side_effects=True, vmem_limit_bytes=40 * 1024 * 1024
        ),
        cost_estimate=pl.CostEstimate(flops=400_000_000, bytes_accessed=5_000_000, transcendentals=0),
    )(occ_irrep.reshape(1, -1), vir_irrep.reshape(1, -1), amplitudes, ladder_ints.T, cycle_ints)
    return ladder.T, cycle


def per_device(amplitudes, ladder_ints, cycle_ints, occ_irrep, vir_irrep):
    fits = jnp.all(vir_irrep[FOLD:] != vir_irrep[:-FOLD])
    return lax.cond(fits, folded_path, dense_path, amplitudes, ladder_ints, cycle_ints, occ_irrep, vir_irrep)


def solution(mesh):
    return jax.shard_map(
        per_device,
        mesh=mesh,
        in_specs=(P("grp", "slab"), P("slab", "grp"), P("grp", None), P(), P()),
        out_specs=(P("grp", "slab"), P("grp", "slab", None)),
        check_vma=False,
    )
```

```python
import functools

import jax
import jax.numpy as jnp
from jax import lax
from jax.experimental import pallas as pl
from jax.experimental.pallas import tpu as pltpu
from jax.sharding import PartitionSpec as P

TILES = 3
IRREPS = 8
MESH = pl.DeviceIdType.MESH


def allowed_mask(lab_i, lab_j, lab_a, lab_b):
    left = jnp.bitwise_xor(lab_i, lab_j)
    right = jnp.bitwise_xor(lab_a, lab_b)
    return left == right


def gather_cols(block):
    groups = lax.axis_size("grp")
    copies = jnp.broadcast_to(block[None], (groups,) + block.shape)
    parts = lax.all_to_all(copies, "grp", split_axis=0, concat_axis=0, tiled=True)
    return jnp.moveaxis(parts, 0, 1).reshape(block.shape[0], groups * block.shape[1])


def sum_parts(partial, axis, dim):
    count = lax.axis_size(axis)
    shape = partial.shape
    split = partial.reshape(shape[:dim] + (count, shape[dim] // count) + shape[dim + 1 :])
    parts = lax.all_to_all(split, axis, split_axis=dim, concat_axis=dim, tiled=True)
    return jnp.sum(parts, axis=dim)


def dense_path(amplitudes, ladder_ints, cycle_ints, occ_irrep, vir_irrep):
    groups = lax.axis_size("grp")
    slabs = lax.axis_size("slab")
    grp_index = lax.axis_index("grp")
    slab_index = lax.axis_index("slab")
    occ_count = occ_irrep.shape[0]
    vir_count = vir_irrep.shape[0]
    occ_local = amplitudes.shape[0] // occ_count
    vir_local = amplitudes.shape[1] // vir_count
    window = ladder_ints.shape[1] * groups
    ladder_cols = window // slabs
    a_count = window // vir_count
    partial_sum = jnp.dot(
        amplitudes,
        gather_cols(ladder_ints),
        precision=lax.Precision.HIGHEST,
        preferred_element_type=jnp.float32,
    )
    ladder = sum_parts(partial_sum, "slab", 1)
    occ_mine = lax.dynamic_slice_in_dim(occ_irrep, grp_index * occ_local, occ_local, 0)
    row_i = jnp.repeat(occ_mine, occ_count)
    row_j = jnp.tile(occ_irrep, occ_local)
    col_a = lax.dynamic_slice_in_dim(
        jnp.repeat(vir_irrep[:a_count], vir_count), slab_index * ladder_cols, ladder_cols, 0
    )
    col_b = lax.dynamic_slice_in_dim(
        jnp.tile(vir_irrep, a_count), slab_index * ladder_cols, ladder_cols, 0
    )
    ladder_keep = allowed_mask(row_i[:, None], row_j[:, None], col_a[None, :], col_b[None, :])
    ladder_term = jnp.where(ladder_keep, ladder, jnp.float32(0.0))
    blocks = amplitudes.reshape(occ_local, occ_count, vir_local, vir_count)
    k_local = cycle_ints.shape[0] // vir_count
    cycle_cols = cycle_ints.shape[1]
    cycle_table = cycle_ints.reshape(k_local, vir_count, cycle_cols)
    regrouped = lax.all_to_all(blocks, "grp", split_axis=1, concat_axis=0, tiled=True)
    partial_cycle = jnp.einsum(
        "ikac,kcw->iaw", regrouped, cycle_table, precision=lax.Precision.HIGHEST
    )
    cycle = sum_parts(partial_cycle, "grp", 0)
    j_count = cycle_cols // vir_count
    vir_mine = lax.dynamic_slice_in_dim(vir_irrep, slab_index * vir_local, vir_local, 0)
    col_j = jnp.repeat(occ_irrep[:j_count], vir_count)
    col_jb = jnp.tile(vir_irrep, j_count)
    cycle_keep = allowed_mask(
        occ_mine[:, None, None],
        col_j[None, None, :],
        vir_mine[None, :, None],
        col_jb[None, None, :],
    )
    cycle_term = jnp.where(cycle_keep, cycle, jnp.float32(0.0))
    return (ladder_term, cycle_term)


def folded_kernel(
    tiles,
    occ_hbm, vir_hbm, amp_hbm, lad_hbm, cyc_hbm, lad_out, cyc_out, run_out,
    occ_v, vir_v, amp, lad, cyc, amp_fold, amp_hi, amp_lo, a2a_send, a2a_recv, cyc_hi, cyc_lo, gath,
    zed, y_recv, z_send, z_recv, quad, lhs_hi, lhs_lo, c_part, c_send, c_recv, c_full,
    load_sem, g_ss, g_rs, a_ss, a_rs, y_ss, y_rs, z_ss, z_rs, q_ss, q_rs, c_ss, c_rs, here_sem, meet_sem,
):
    f32, i32, bf16 = jnp.float32, jnp.int32, jnp.bfloat16
    g, s = lax.axis_index("grp"), lax.axis_index("slab")
    core, x, y = g % 2, (g // 2) % 4, g // 8
    z, half = s // 2, s % 2

    load_l = pltpu.make_async_copy(lad_hbm, lad, load_sem.at[0])
    load_a = pltpu.make_async_copy(amp_hbm, amp, load_sem.at[1])
    load_w = pltpu.make_async_copy(cyc_hbm, cyc, load_sem.at[2])
    load_o = pltpu.make_async_copy(occ_hbm, occ_v, load_sem.at[3])
    load_v = pltpu.make_async_copy(vir_hbm, vir_v, load_sem.at[4])
    load_l.start()
    load_o.start()
    load_v.start()
    load_a.start()
    load_w.start()

    barrier = pltpu.get_barrier_semaphore()

    @pl.loop(1, 16)
    def _(r):
        to = (g + r) % 16

        @pl.when(to != 0)
        def _():
            pl.semaphore_signal(barrier, inc=1, device_id=(to, s), device_id_type=MESH)

    def iota(shape, dim):
        return lax.broadcasted_iota(i32, shape, dim)

    def split(value):
        high = value.astype(bf16)
        return high, (value - high.astype(f32)).astype(bf16)

    low64 = iota((1, 128), 1) < 64
    lane = iota((1, 128), 1)

    def pack_pair(first, second):
        keep = jnp.where(low64, first, second)
        move = jnp.where(low64, second, first)
        return keep + pltpu.roll(move, 64, 1)

    def spread(rows):
        turned = [row if n == 0 else pltpu.roll(row, 16 * n, 1) for n, row in enumerate(rows)]
        for bit in (1, 2, 4):
            here = (lane // 16) // bit % 2 == 1
            turned = [jnp.where(here, turned[(n + bit) % 8], turned[n]) for n in range(8)]
        return [turned[0]] + [pltpu.roll(turned[8 - p], 128 - 16 * p, 1) for p in range(1, 8)]

    def fold(src, rows):
        sums = [None] * tiles
        for part in range(2):
            runs = spread([src[rows, 256 * n + 128 * part : 256 * n + 128 * part + 128] for n in range(8)])
            for p in range(8):
                u = (8 * part + p) % tiles
                sums[u] = runs[p] if sums[u] is None else sums[u] + runs[p]
        return sums

    def regroup(src, dst, blocks):
        low4 = iota((8, 1), 0) < 4

        @pl.loop(0, 8)
        def _(q):
            for n in range(0, blocks, 2):
                for c in range(src.shape[1] // 128):
                    cols = slice(128 * c, 128 * c + 128)
                    one = src[pl.ds(pl.multiple_of(64 * n + 8 * q, 8), 8), cols]
                    two = src[pl.ds(pl.multiple_of(64 * n + 64 + 8 * q, 8), 8), cols]
                    dst[2 * q, c, 4 * n : 4 * n + 8, :] = jnp.where(low4, one, pltpu.roll(two, 4, 0))
                    dst[2 * q + 1, c, 4 * n : 4 * n + 8, :] = jnp.where(low4, pltpu.roll(one, 4, 0), two)

    load_l.wait()

    @pl.loop(0, 4)
    def _(r):
        rows = pl.ds(pl.multiple_of(16 * r, 16), 16)
        for u, folded in enumerate(fold(lad, rows)):
            gath[g, rows, 128 * u : 128 * u + 128] = folded

    @pl.when(g != 0)
    def _():
        pl.semaphore_wait(barrier, 15)

    @pl.when(g == 1)
    def _():
        pl.semaphore_signal(here_sem, inc=1, device_id=(0, s), device_id_type=MESH)

    @pl.when(g == 0)
    def _():
        pl.semaphore_wait(here_sem, 1)

        @pl.loop(1, 32)
        def _(r):
            pl.semaphore_signal(barrier, inc=1, device_id=(0, (s + r) % 32), device_id_type=MESH)

    def meet_slabs():
        @pl.when(g == 0)
        def _():
            pl.semaphore_wait(barrier, 31)

            @pl.loop(1, 16)
            def _(r):
                pl.semaphore_signal(meet_sem, inc=1, device_id=(r, s), device_id_type=MESH)

        @pl.when(g != 0)
        def _():
            pl.semaphore_wait(meet_sem, 1)

    def dev(y_, x_, core_):
        return (y_ * 4 + x_ % 4) * 2 + core_

    turn = 1 - 2 * (x % 2)
    sib, y_dev = dev(y, x, 1 - core), dev(1 - y, x, core)
    mate, other = dev(y, x + 4 + turn, core), dev(y, x + 4 - turn, core)
    y_mate, y_other = dev(1 - y, x + 4 + turn, core), dev(1 - y, x + 4 - turn, core)
    across, y_across = dev(y, x + 2, core), dev(1 - y, x + 2, core)

    def g_copy(k, slot, to, rows=None):
        ref = gath.at[slot] if rows is None else gath.at[slot, rows]
        return pltpu.make_async_remote_copy(
            src_ref=ref, dst_ref=ref, send_sem=g_ss.at[k], recv_sem=g_rs.at[k],
            device_id=(to, s), device_id_type=MESH,
        )

    lower, upper = pl.ds(0, 32), pl.ds(32, 32)
    moves = [
        g_copy(0, g, y_dev), g_copy(1, g, mate), g_copy(2, g, other), g_copy(3, g, sib),
        g_copy(4, y_dev, mate), g_copy(5, y_dev, other), g_copy(6, y_dev, sib),
        g_copy(7, mate, other, lower), g_copy(8, other, mate, upper),
        g_copy(9, y_mate, other, lower), g_copy(10, y_other, mate, upper),
        g_copy(11, mate, sib), g_copy(12, other, sib), g_copy(13, y_mate, sib), g_copy(14, y_other, sib),
        g_copy(15, across, sib), g_copy(16, y_across, sib),
    ]

    def go(*numbers):
        for k in numbers:
            moves[k].start()

    def got(*numbers):
        for k in numbers:
            moves[k].wait_recv()

    go(0, 1, 2, 3)

    load_a.wait()

    @pl.loop(0, 16)
    def _(r):
        rows = pl.ds(pl.multiple_of(16 * r, 16), 16)
        for u, folded in enumerate(fold(amp, rows)):
            cols = slice(128 * u, 128 * u + 128)
            amp_fold[rows, cols] = folded
            amp_hi[rows, cols], amp_lo[rows, cols] = split(folded)

    regroup(amp_fold, a2a_send, 4)
    got(0)
    go(4, 5, 6)
    got(1)
    go(7, 11)
    got(2)
    go(8, 12)

    mine16 = pl.ds(pl.multiple_of(16 * g, 16), 16)

    def a_copy(r):
        to = (g + r) % 16
        return pltpu.make_async_remote_copy(
            src_ref=a2a_send.at[to], dst_ref=a2a_recv.at[:, mine16],
            send_sem=a_ss.at[r], recv_sem=a_rs.at[r], device_id=(to, s), device_id_type=MESH,
        )

    @pl.loop(1, 16)
    def _(r):
        a_copy(r).start()

    a2a_recv[:, mine16, :] = a2a_send[g]

    load_o.wait()
    load_v.wait()

    def run_starts(ref):
        return [
            jnp.sum(jnp.where(ref[...] < v, 1.0, 0.0), axis=1, keepdims=True).astype(i32) for v in range(1, IRREPS)
        ]

    occ_starts, vir_starts = run_starts(occ_v), run_starts(vir_v)

    starts = [0] + vir_starts + [vir_v.shape[1]]
    longest = starts[1]
    for v in range(1, IRREPS):
        longest = jnp.maximum(longest, starts[v + 1] - starts[v])
    run_out[0, 0] = jnp.max(longest)

    def label(index, starts):
        total = jnp.where(index >= starts[0], 1, 0)
        for start in starts[1:]:
            total = total + jnp.where(index >= start, 1, 0)
        return total

    def occ_label(index):
        return label(index, occ_starts)

    def vir_label(index):
        return label(index, vir_starts)

    zero = jnp.zeros((1, 128), i32)

    def pair_label(part):
        return occ_label(4 * g + 2 * part + lane // 64) ^ occ_label(lane % 64)

    ij_label = [pair_label(part) for part in range(2)]
    row_label = [vir_label(iota((64, 128), 0) + 64 * m) for m in range(4)]

    def dot(first, second, dims):
        return lax.dot_general(first, second, (dims, ((), ())), preferred_element_type=f32)

    def dot3(a_hi, a_lo, b_hi, b_lo, dims):
        return dot(a_hi, b_hi, dims) + (dot(a_hi, b_lo, dims) + dot(a_lo, b_hi, dims))

    order = [2 * y + x // 2, 2 * (1 - y) + x // 2, 2 * y + 1 - x // 2, 2 * (1 - y) + 1 - x // 2]

    def y_copy(n):
        return pltpu.make_async_remote_copy(
            src_ref=zed.at[1 - half, order[n]], dst_ref=y_recv.at[order[n]],
            send_sem=y_ss.at[n], recv_sem=y_rs.at[n],
            device_id=(g, z * 2 + (1 - half)), device_id_type=MESH,
        )

    def z_copy(to):
        r = (to - z + 16) % 16
        return pltpu.make_async_remote_copy(
            src_ref=z_send.at[to], dst_ref=z_recv.at[z],
            send_sem=z_ss.at[r], recv_sem=z_rs.at[r], device_id=(g, to * 2 + half), device_id_type=MESH,
        )

    def ladder_product(n):
        a = order[n]
        hi, lo = split(gath[pl.ds(4 * a, 4)].reshape(256, 128 * tiles))
        product = dot3(hi, lo, amp_hi[...], amp_lo[...], ((1,), (1,)))
        a_label = vir_label(zero + a)
        for part in range(2):
            cols = slice(128 * part, 128 * part + 128)
            want = ij_label[part] ^ a_label
            total = jnp.where(row_label[0] == want, product[0:64, cols], f32(0.0))
            for m in range(1, 4):
                total = total + jnp.where(row_label[m] == want, product[64 * m : 64 * m + 64, cols], f32(0.0))
            zed[0, a, :, cols] = total[0:32]
            zed[1, a, :, cols] = total[32:64]
        y_copy(n).start()

    def ladder_sums(n):
        a = order[n]
        y_copy(n).wait_recv()
        total = zed[half, a] + y_recv[a]
        for q in range(4):
            z_send[4 * a + q] = total[8 * q : 8 * q + 8]
            to = 4 * a + q

            @pl.when(to != z)
            def _():
                z_copy(to).start()

    got(3, 11)
    meet_slabs()
    ladder_product(0)
    got(4)
    go(9, 13)
    got(5)
    go(10, 14)

    load_w.wait()

    @pl.loop(0, 4)
    def _(k):
        for u in range(tiles):
            part = cyc[pl.ds(pl.multiple_of(256 * k + 16 * u, 16), 16), :]
            for e in range(u + tiles, 16, tiles):
                part = part + cyc[pl.ds(pl.multiple_of(256 * k + 16 * e, 16), 16), :]
            rows = pl.ds(pl.multiple_of(16 * (tiles * k + u), 16), 16)
            cyc_hi[rows, :], cyc_lo[rows, :] = split(part)

    if tiles < 4:
        cyc_hi[64 * tiles : 256, :] = jnp.zeros((256 - 64 * tiles, 512), bf16)
        cyc_lo[64 * tiles : 256, :] = jnp.zeros((256 - 64 * tiles, 512), bf16)

    got(7, 8)
    go(15)
    got(6, 13)
    ladder_product(1)
    got(9, 10)
    go(16)

    ladder_sums(0)
    got(12, 15)
    ladder_product(2)
    ladder_sums(1)
    got(14, 16)
    ladder_product(3)
    ladder_sums(2)
    ladder_sums(3)
    z_recv[z] = z_send[z]

    @pl.loop(1, 16)
    def _(r):
        a_copy(r).wait_recv()

    for r in range(4):
        for w in range(2):
            pieces = []
            for q in range(8 * w, 8 * w + 8):
                k, u = q // tiles, q % tiles
                if k < 4:
                    pieces.append(a2a_recv[u, pl.ds(64 * r + k, 16, stride=4), :])
                else:
                    pieces.append(jnp.zeros((16, 128), f32))
            cols = slice(128 * w, 128 * w + 128)
            for a, value in enumerate(spread(pieces)):
                at = slice(64 * a + 16 * r, 64 * a + 16 * r + 16)
                lhs_hi[at, cols], lhs_lo[at, cols] = split(value)

    jb_label = [
        occ_label(zero + part // 2) ^ vir_label(lane + 128 * (part % 2)) for part in range(4)
    ]

    @pl.loop(0, 2)
    def _(h):
        rows = pl.ds(pl.multiple_of(256 * h, 256), 256)
        r_id = iota((256, 128), 0)
        ia_label = occ_label(r_id % 64) ^ vir_label(8 * s + 4 * h + r_id // 64)
        folds = []
        for j in range(2):
            cols = slice(256 * j, 256 * j + 256)
            product = dot3(lhs_hi[rows, :], lhs_lo[rows, :], cyc_hi[:, cols], cyc_lo[:, cols], ((1,), (0,)))
            kept = [
                jnp.where(ia_label == jb_label[2 * j + part], product[:, 128 * part : 128 * part + 128], f32(0.0))
                for part in range(2)
            ]
            folds.append(kept[0] + kept[1])
        c_part[rows, :] = pack_pair(folds[0], folds[1])

    regroup(c_part, c_send, 8)

    def c_copy(r):
        to = (g + r) % 16
        return pltpu.make_async_remote_copy(
            src_ref=c_send.at[to, 0], dst_ref=c_recv.at[g],
            send_sem=c_ss.at[r], recv_sem=c_rs.at[r], device_id=(to, s), device_id_type=MESH,
        )

    @pl.loop(1, 16)
    def _(r):
        c_copy(r).start()

    c_recv[g] = c_send[g, 0]

    def z_arrival(r):
        return pltpu.make_async_remote_copy(
            src_ref=z_send.at[z], dst_ref=z_recv.at[z], send_sem=z_ss.at[r], recv_sem=z_rs.at[r],
            device_id=(g, ((z + r) % 16) * 2 + half), device_id_type=MESH,
        )

    @pl.loop(1, 16)
    def _(r):
        z_arrival(r).wait_recv()

    total = z_recv[0]
    for n in range(1, 16):
        total = total + z_recv[n]
    quarter = z % 4
    quad[quarter] = total

    def q_copy(d):
        to = 4 * (z // 4) + (z + d) % 4
        return pltpu.make_async_remote_copy(
            src_ref=quad.at[quarter], dst_ref=quad.at[quarter],
            send_sem=q_ss.at[d], recv_sem=q_rs.at[d], device_id=(g, to * 2 + half), device_id_type=MESH,
        )

    for d in range(1, 4):
        q_copy(d).start()

    @pl.loop(1, 16)
    def _(r):
        c_copy(r).wait_recv()

    total = c_recv[0]
    for n in range(1, 16):
        total = total + c_recv[n]
    turned = pltpu.roll(total, 64, 1)
    both = [jnp.where(low64, total, turned), jnp.where(low64, turned, total)]
    r_id = iota((32, 128), 0)
    ia_label = occ_label(4 * g + r_id % 4) ^ vir_label(8 * s + r_id // 4)
    for part in range(4):
        c_full[part] = jnp.where(ia_label == jb_label[part], both[part // 2], f32(0.0))
    for i in range(4):
        for part in range(4):
            cyc_out[i, :, 128 * part : 128 * part + 128] = c_full[part, pl.ds(i, 8, stride=4), :]

    for d in range(1, 4):
        q_copy(d).wait_recv()

    b_label = vir_label(zero + z // 4) ^ vir_label(32 * (s % 8) + iota((32, 128), 0))
    full = quad[...].reshape(32, 256)
    for part in range(2):
        cols = slice(128 * part, 128 * part + 128)
        lad_out[:, cols] = jnp.where(ij_label[part] == b_label, full[:, cols], f32(0.0))

    for move in moves:
        move.wait_send()
    for d in range(1, 4):
        q_copy(d).wait_send()

    for n in range(4):
        y_copy(n).wait_send()

    @pl.loop(1, 16)
    def _(r):
        a_copy(r).wait_send()
        c_copy(r).wait_send()
        z_arrival(r).wait_send()


def folded_path(tiles, amplitudes, ladder_ints, cycle_ints, occ_irrep, vir_irrep):
    f32, bf16 = jnp.float32, jnp.bfloat16
    vmem = pltpu.VMEM
    dma = pltpu.SemaphoreType.DMA
    ladder, cycle, longest = pl.pallas_call(
        functools.partial(folded_kernel, tiles),
        out_shape=(
            jax.ShapeDtypeStruct((32, 256), f32),
            jax.ShapeDtypeStruct((4, 8, 512), f32),
            jax.ShapeDtypeStruct((1, 1), jnp.int32),
        ),
        in_specs=[pl.BlockSpec(memory_space=pl.ANY)] * 5,
        out_specs=[pl.BlockSpec(memory_space=pltpu.VMEM)] * 2 + [pl.BlockSpec(memory_space=pltpu.SMEM)],
        scratch_shapes=[
            vmem((1, 64), jnp.int32), vmem((1, 256), jnp.int32),
            vmem((256, 2048), f32), vmem((64, 2048), f32), vmem((1024, 512), f32),
            vmem((256, 128 * tiles), f32), vmem((256, 128 * tiles), bf16), vmem((256, 128 * tiles), bf16),
            vmem((16, tiles, 16, 128), f32), vmem((tiles, 256, 128), f32),
            vmem((256, 512), bf16), vmem((256, 512), bf16), vmem((16, 64, 128 * tiles), f32),
            vmem((2, 4, 32, 256), f32), vmem((4, 32, 256), f32), vmem((16, 8, 256), f32), vmem((16, 8, 256), f32),
            vmem((4, 8, 256), f32), vmem((512, 256), bf16), vmem((512, 256), bf16),
            vmem((512, 128), f32), vmem((16, 1, 32, 128), f32), vmem((16, 32, 128), f32), vmem((4, 32, 128), f32),
            dma((5,)), dma((17,)), dma((17,)), dma((16,)), dma((16,)), dma((4,)), dma((4,)),
            dma((16,)), dma((16,)), dma((4,)), dma((4,)), dma((16,)), dma((16,)),
            pltpu.SemaphoreType.REGULAR, pltpu.SemaphoreType.REGULAR,
        ],
        compiler_params=pltpu.CompilerParams(
            collective_id=0, has_side_effects=True, vmem_limit_bytes=56 * 1024 * 1024
        ),
        cost_estimate=pl.CostEstimate(flops=400_000_000, bytes_accessed=5_000_000, transcendentals=0),
    )(occ_irrep.reshape(1, -1), vir_irrep.reshape(1, -1), amplitudes, ladder_ints.T, cycle_ints)
    return ladder.T, cycle, longest[0, 0]


def per_device(amplitudes, ladder_ints, cycle_ints, occ_irrep, vir_irrep):
    ladder, cycle, longest = folded_path(TILES, amplitudes, ladder_ints, cycle_ints, occ_irrep, vir_irrep)
    return lax.cond(
        longest <= 16 * TILES,
        lambda: (ladder, cycle),
        lambda: dense_path(amplitudes, ladder_ints, cycle_ints, occ_irrep, vir_irrep),
    )


def solution(mesh):
    return jax.shard_map(
        per_device,
        mesh=mesh,
        in_specs=(P("grp", "slab"), P("slab", "grp"), P("grp", None), P(), P()),
        out_specs=(P("grp", "slab"), P("grp", "slab", None)),
        check_vma=False,
    )
```

```python
import functools

import jax
import jax.numpy as jnp
from jax import lax
from jax.experimental import pallas as pl
from jax.experimental.pallas import tpu as pltpu
from jax.sharding import PartitionSpec as P

TILES = 3
IRREPS = 8
MESH = pl.DeviceIdType.MESH


def allowed_mask(lab_i, lab_j, lab_a, lab_b):
    left = jnp.bitwise_xor(lab_i, lab_j)
    right = jnp.bitwise_xor(lab_a, lab_b)
    return left == right


def gather_cols(block):
    groups = lax.axis_size("grp")
    copies = jnp.broadcast_to(block[None], (groups,) + block.shape)
    parts = lax.all_to_all(copies, "grp", split_axis=0, concat_axis=0, tiled=True)
    return jnp.moveaxis(parts, 0, 1).reshape(block.shape[0], groups * block.shape[1])


def sum_parts(partial, axis, dim):
    count = lax.axis_size(axis)
    shape = partial.shape
    split = partial.reshape(shape[:dim] + (count, shape[dim] // count) + shape[dim + 1 :])
    parts = lax.all_to_all(split, axis, split_axis=dim, concat_axis=dim, tiled=True)
    return jnp.sum(parts, axis=dim)


def dense_path(amplitudes, ladder_ints, cycle_ints, occ_irrep, vir_irrep):
    groups = lax.axis_size("grp")
    slabs = lax.axis_size("slab")
    grp_index = lax.axis_index("grp")
    slab_index = lax.axis_index("slab")
    occ_count = occ_irrep.shape[0]
    vir_count = vir_irrep.shape[0]
    occ_local = amplitudes.shape[0] // occ_count
    vir_local = amplitudes.shape[1] // vir_count
    window = ladder_ints.shape[1] * groups
    ladder_cols = window // slabs
    a_count = window // vir_count
    partial_sum = jnp.dot(
        amplitudes,
        gather_cols(ladder_ints),
        precision=lax.Precision.HIGHEST,
        preferred_element_type=jnp.float32,
    )
    ladder = sum_parts(partial_sum, "slab", 1)
    occ_mine = lax.dynamic_slice_in_dim(occ_irrep, grp_index * occ_local, occ_local, 0)
    row_i = jnp.repeat(occ_mine, occ_count)
    row_j = jnp.tile(occ_irrep, occ_local)
    col_a = lax.dynamic_slice_in_dim(
        jnp.repeat(vir_irrep[:a_count], vir_count), slab_index * ladder_cols, ladder_cols, 0
    )
    col_b = lax.dynamic_slice_in_dim(
        jnp.tile(vir_irrep, a_count), slab_index * ladder_cols, ladder_cols, 0
    )
    ladder_keep = allowed_mask(row_i[:, None], row_j[:, None], col_a[None, :], col_b[None, :])
    ladder_term = jnp.where(ladder_keep, ladder, jnp.float32(0.0))
    blocks = amplitudes.reshape(occ_local, occ_count, vir_local, vir_count)
    k_local = cycle_ints.shape[0] // vir_count
    cycle_cols = cycle_ints.shape[1]
    cycle_table = cycle_ints.reshape(k_local, vir_count, cycle_cols)
    regrouped = lax.all_to_all(blocks, "grp", split_axis=1, concat_axis=0, tiled=True)
    partial_cycle = jnp.einsum(
        "ikac,kcw->iaw", regrouped, cycle_table, precision=lax.Precision.HIGHEST
    )
    cycle = sum_parts(partial_cycle, "grp", 0)
    j_count = cycle_cols // vir_count
    vir_mine = lax.dynamic_slice_in_dim(vir_irrep, slab_index * vir_local, vir_local, 0)
    col_j = jnp.repeat(occ_irrep[:j_count], vir_count)
    col_jb = jnp.tile(vir_irrep, j_count)
    cycle_keep = allowed_mask(
        occ_mine[:, None, None],
        col_j[None, None, :],
        vir_mine[None, :, None],
        col_jb[None, None, :],
    )
    cycle_term = jnp.where(cycle_keep, cycle, jnp.float32(0.0))
    return (ladder_term, cycle_term)


def folded_kernel(
    tiles,
    occ_hbm, vir_hbm, amp_hbm, lad_hbm, cyc_hbm, lad_out, cyc_out, run_out,
    occ_v, vir_v, amp, lad, cyc, amp_fold, amp_hi, amp_lo, a2a_send, a2a_recv, cyc_hi, cyc_lo, gath,
    zed, y_recv, z_send, z_recv, quad, lhs_hi, lhs_lo, c_part, c_send, c_recv, c_full,
    load_sem, g_ss, g_rs, a_ss, a_rs, y_ss, y_rs, z_ss, z_rs, q_ss, q_rs, c_ss, c_rs, here_sem, meet_sem,
):
    f32, i32, bf16 = jnp.float32, jnp.int32, jnp.bfloat16
    g, s = lax.axis_index("grp"), lax.axis_index("slab")
    core, x, y = g % 2, (g // 2) % 4, g // 8
    z, half = s // 2, s % 2

    load_l = pltpu.make_async_copy(lad_hbm, lad, load_sem.at[0])
    load_a = pltpu.make_async_copy(amp_hbm, amp, load_sem.at[1])
    load_w = pltpu.make_async_copy(cyc_hbm, cyc, load_sem.at[2])
    load_o = pltpu.make_async_copy(occ_hbm, occ_v, load_sem.at[3])
    load_v = pltpu.make_async_copy(vir_hbm, vir_v, load_sem.at[4])
    load_l.start()
    load_o.start()
    load_v.start()
    load_a.start()
    load_w.start()

    barrier = pltpu.get_barrier_semaphore()

    @pl.loop(1, 16)
    def _(r):
        to = (g + r) % 16

        @pl.when(to != 0)
        def _():
            pl.semaphore_signal(barrier, inc=1, device_id=(to, s), device_id_type=MESH)

    def iota(shape, dim):
        return lax.broadcasted_iota(i32, shape, dim)

    def split(value):
        high = value.astype(bf16)
        return high, (value - high.astype(f32)).astype(bf16)

    low64 = iota((1, 128), 1) < 64
    lane = iota((1, 128), 1)

    def pack_pair(first, second):
        keep = jnp.where(low64, first, second)
        move = jnp.where(low64, second, first)
        return keep + pltpu.roll(move, 64, 1)

    def spread(rows):
        turned = [row if n == 0 else pltpu.roll(row, 16 * n, 1) for n, row in enumerate(rows)]
        for bit in (1, 2, 4):
            here = (lane // 16) // bit % 2 == 1
            turned = [jnp.where(here, turned[(n + bit) % 8], turned[n]) for n in range(8)]
        return [turned[0]] + [pltpu.roll(turned[8 - p], 128 - 16 * p, 1) for p in range(1, 8)]

    def fold(src, rows):
        sums = [None] * tiles
        for part in range(2):
            runs = spread([src[rows, 256 * n + 128 * part : 256 * n + 128 * part + 128] for n in range(8)])
            for p in range(8):
                u = (8 * part + p) % tiles
                sums[u] = runs[p] if sums[u] is None else sums[u] + runs[p]
        return sums

    def regroup(src, dst, blocks):
        low4 = iota((8, 1), 0) < 4

        @pl.loop(0, 8)
        def _(q):
            for n in range(0, blocks, 2):
                for c in range(src.shape[1] // 128):
                    cols = slice(128 * c, 128 * c + 128)
                    one = src[pl.ds(pl.multiple_of(64 * n + 8 * q, 8), 8), cols]
                    two = src[pl.ds(pl.multiple_of(64 * n + 64 + 8 * q, 8), 8), cols]
                    dst[2 * q, c, 4 * n : 4 * n + 8, :] = jnp.where(low4, one, pltpu.roll(two, 4, 0))
                    dst[2 * q + 1, c, 4 * n : 4 * n + 8, :] = jnp.where(low4, pltpu.roll(one, 4, 0), two)

    load_l.wait()

    @pl.loop(0, 4)
    def _(r):
        rows = pl.ds(pl.multiple_of(16 * r, 16), 16)
        for u, folded in enumerate(fold(lad, rows)):
            gath[g, rows, 128 * u : 128 * u + 128] = folded

    @pl.when(g != 0)
    def _():
        pl.semaphore_wait(barrier, 15)

    @pl.when(g == 1)
    def _():
        pl.semaphore_signal(here_sem, inc=1, device_id=(0, s), device_id_type=MESH)

    @pl.when(g == 0)
    def _():
        pl.semaphore_wait(here_sem, 1)

        @pl.loop(1, 32)
        def _(r):
            pl.semaphore_signal(barrier, inc=1, device_id=(0, (s + r) % 32), device_id_type=MESH)

    def meet_slabs():
        @pl.when(g == 0)
        def _():
            pl.semaphore_wait(barrier, 31)

            @pl.loop(1, 16)
            def _(r):
                pl.semaphore_signal(meet_sem, inc=1, device_id=(r, s), device_id_type=MESH)

        @pl.when(g != 0)
        def _():
            pl.semaphore_wait(meet_sem, 1)

    def dev(y_, x_, core_):
        return (y_ * 4 + x_ % 4) * 2 + core_

    turn = 1 - 2 * (x % 2)
    sib, y_dev = dev(y, x, 1 - core), dev(1 - y, x, core)
    mate, other = dev(y, x + 4 + turn, core), dev(y, x + 4 - turn, core)
    y_mate, y_other = dev(1 - y, x + 4 + turn, core), dev(1 - y, x + 4 - turn, core)
    across, y_across = dev(y, x + 2, core), dev(1 - y, x + 2, core)

    def g_copy(k, slot, to, rows=None):
        ref = gath.at[slot] if rows is None else gath.at[slot, rows]
        return pltpu.make_async_remote_copy(
            src_ref=ref, dst_ref=ref, send_sem=g_ss.at[k], recv_sem=g_rs.at[k],
            device_id=(to, s), device_id_type=MESH,
        )

    lower, upper = pl.ds(0, 32), pl.ds(32, 32)
    moves = [
        g_copy(0, g, y_dev), g_copy(1, g, mate), g_copy(2, g, other), g_copy(3, g, sib),
        g_copy(4, y_dev, mate), g_copy(5, y_dev, other), g_copy(6, y_dev, sib),
        g_copy(7, mate, other, lower), g_copy(8, other, mate, upper),
        g_copy(9, y_mate, other, lower), g_copy(10, y_other, mate, upper),
        g_copy(11, mate, sib), g_copy(12, other, sib), g_copy(13, y_mate, sib), g_copy(14, y_other, sib),
        g_copy(15, across, sib), g_copy(16, y_across, sib),
    ]

    def go(*numbers):
        for k in numbers:
            moves[k].start()

    def got(*numbers):
        for k in numbers:
            moves[k].wait_recv()

    go(0, 1, 2, 3)

    load_a.wait()

    @pl.loop(0, 16)
    def _(r):
        rows = pl.ds(pl.multiple_of(16 * r, 16), 16)
        for u, folded in enumerate(fold(amp, rows)):
            cols = slice(128 * u, 128 * u + 128)
            amp_fold[rows, cols] = folded
            amp_hi[rows, cols], amp_lo[rows, cols] = split(folded)

    got(0)
    go(4, 5, 6)
    got(1)
    go(7, 11)
    got(2)
    go(8, 12)

    regroup(amp_fold, a2a_send, 4)
    mine16 = pl.ds(pl.multiple_of(16 * g, 16), 16)

    def a_copy(r):
        to = (g + r) % 16
        return pltpu.make_async_remote_copy(
            src_ref=a2a_send.at[to], dst_ref=a2a_recv.at[:, mine16],
            send_sem=a_ss.at[r], recv_sem=a_rs.at[r], device_id=(to, s), device_id_type=MESH,
        )

    load_o.wait()
    load_v.wait()

    def run_starts(ref):
        return [
            jnp.sum(jnp.where(ref[...] < v, 1.0, 0.0), axis=1, keepdims=True).astype(i32) for v in range(1, IRREPS)
        ]

    occ_starts, vir_starts = run_starts(occ_v), run_starts(vir_v)

    starts = [0] + vir_starts + [vir_v.shape[1]]
    longest = starts[1]
    for v in range(1, IRREPS):
        longest = jnp.maximum(longest, starts[v + 1] - starts[v])
    run_out[0, 0] = jnp.max(longest)

    def label(index, starts):
        total = jnp.where(index >= starts[0], 1, 0)
        for start in starts[1:]:
            total = total + jnp.where(index >= start, 1, 0)
        return total

    def occ_label(index):
        return label(index, occ_starts)

    def vir_label(index):
        return label(index, vir_starts)

    zero = jnp.zeros((1, 128), i32)

    def pair_label(part):
        return occ_label(4 * g + 2 * part + lane // 64) ^ occ_label(lane % 64)

    ij_label = [pair_label(part) for part in range(2)]
    row_label = [vir_label(iota((64, 128), 0) + 64 * m) for m in range(4)]

    def dot(first, second, dims):
        return lax.dot_general(first, second, (dims, ((), ())), preferred_element_type=f32)

    def dot3(a_hi, a_lo, b_hi, b_lo, dims):
        return dot(a_hi, b_hi, dims) + (dot(a_hi, b_lo, dims) + dot(a_lo, b_hi, dims))

    order = [2 * y + x // 2, 2 * (1 - y) + x // 2, 2 * y + 1 - x // 2, 2 * (1 - y) + 1 - x // 2]

    def y_copy(n):
        return pltpu.make_async_remote_copy(
            src_ref=zed.at[1 - half, order[n]], dst_ref=y_recv.at[order[n]],
            send_sem=y_ss.at[n], recv_sem=y_rs.at[n],
            device_id=(g, z * 2 + (1 - half)), device_id_type=MESH,
        )

    def z_copy(to):
        r = (to - z + 16) % 16
        return pltpu.make_async_remote_copy(
            src_ref=z_send.at[to], dst_ref=z_recv.at[z],
            send_sem=z_ss.at[r], recv_sem=z_rs.at[r], device_id=(g, to * 2 + half), device_id_type=MESH,
        )

    def ladder_product(n):
        a = order[n]
        hi, lo = split(gath[pl.ds(4 * a, 4)].reshape(256, 128 * tiles))
        product = dot3(hi, lo, amp_hi[...], amp_lo[...], ((1,), (1,)))
        a_label = vir_label(zero + a)
        for part in range(2):
            cols = slice(128 * part, 128 * part + 128)
            want = ij_label[part] ^ a_label
            total = jnp.where(row_label[0] == want, product[0:64, cols], f32(0.0))
            for m in range(1, 4):
                total = total + jnp.where(row_label[m] == want, product[64 * m : 64 * m + 64, cols], f32(0.0))
            zed[0, a, :, cols] = total[0:32]
            zed[1, a, :, cols] = total[32:64]
        y_copy(n).start()

    def ladder_sums(n):
        a = order[n]
        y_copy(n).wait_recv()
        total = zed[half, a] + y_recv[a]
        for q in range(4):
            z_send[4 * a + q] = total[8 * q : 8 * q + 8]
            to = 4 * a + q

            @pl.when(to != z)
            def _():
                z_copy(to).start()

    got(3, 11)
    meet_slabs()
    ladder_product(0)
    got(4)
    go(9, 13)
    got(5)
    go(10, 14)

    load_w.wait()

    @pl.loop(0, 4)
    def _(k):
        for u in range(tiles):
            part = cyc[pl.ds(pl.multiple_of(256 * k + 16 * u, 16), 16), :]
            for e in range(u + tiles, 16, tiles):
                part = part + cyc[pl.ds(pl.multiple_of(256 * k + 16 * e, 16), 16), :]
            rows = pl.ds(pl.multiple_of(16 * (tiles * k + u), 16), 16)
            cyc_hi[rows, :], cyc_lo[rows, :] = split(part)

    if tiles < 4:
        cyc_hi[64 * tiles : 256, :] = jnp.zeros((256 - 64 * tiles, 512), bf16)
        cyc_lo[64 * tiles : 256, :] = jnp.zeros((256 - 64 * tiles, 512), bf16)

    got(7, 8)
    go(15)
    got(6, 13)
    ladder_product(1)
    got(9, 10)
    go(16)

    @pl.loop(1, 16)
    def _(r):
        a_copy(r).start()

    a2a_recv[:, mine16, :] = a2a_send[g]

    ladder_sums(0)
    got(12, 15)
    ladder_product(2)
    ladder_sums(1)
    got(14, 16)
    ladder_product(3)
    ladder_sums(2)
    ladder_sums(3)
    z_recv[z] = z_send[z]

    @pl.loop(1, 16)
    def _(r):
        a_copy(r).wait_recv()

    for r in range(4):
        for w in range(2):
            pieces = []
            for q in range(8 * w, 8 * w + 8):
                k, u = q // tiles, q % tiles
                if k < 4:
                    pieces.append(a2a_recv[u, pl.ds(64 * r + k, 16, stride=4), :])
                else:
                    pieces.append(jnp.zeros((16, 128), f32))
            cols = slice(128 * w, 128 * w + 128)
            for a, value in enumerate(spread(pieces)):
                at = slice(64 * a + 16 * r, 64 * a + 16 * r + 16)
                lhs_hi[at, cols], lhs_lo[at, cols] = split(value)

    jb_label = [
        occ_label(zero + part // 2) ^ vir_label(lane + 128 * (part % 2)) for part in range(4)
    ]

    @pl.loop(0, 2)
    def _(h):
        rows = pl.ds(pl.multiple_of(256 * h, 256), 256)
        r_id = iota((256, 128), 0)
        ia_label = occ_label(r_id % 64) ^ vir_label(8 * s + 4 * h + r_id // 64)
        folds = []
        for j in range(2):
            cols = slice(256 * j, 256 * j + 256)
            product = dot3(lhs_hi[rows, :], lhs_lo[rows, :], cyc_hi[:, cols], cyc_lo[:, cols], ((1,), (0,)))
            kept = [
                jnp.where(ia_label == jb_label[2 * j + part], product[:, 128 * part : 128 * part + 128], f32(0.0))
                for part in range(2)
            ]
            folds.append(kept[0] + kept[1])
        c_part[rows, :] = pack_pair(folds[0], folds[1])

    regroup(c_part, c_send, 8)

    def c_copy(r):
        to = (g + r) % 16
        return pltpu.make_async_remote_copy(
            src_ref=c_send.at[to, 0], dst_ref=c_recv.at[g],
            send_sem=c_ss.at[r], recv_sem=c_rs.at[r], device_id=(to, s), device_id_type=MESH,
        )

    @pl.loop(1, 16)
    def _(r):
        c_copy(r).start()

    c_recv[g] = c_send[g, 0]

    def z_arrival(r):
        return pltpu.make_async_remote_copy(
            src_ref=z_send.at[z], dst_ref=z_recv.at[z], send_sem=z_ss.at[r], recv_sem=z_rs.at[r],
            device_id=(g, ((z + r) % 16) * 2 + half), device_id_type=MESH,
        )

    @pl.loop(1, 16)
    def _(r):
        z_arrival(r).wait_recv()

    total = z_recv[0]
    for n in range(1, 16):
        total = total + z_recv[n]
    quarter = z % 4
    quad[quarter] = total

    def q_copy(d):
        to = 4 * (z // 4) + (z + d) % 4
        return pltpu.make_async_remote_copy(
            src_ref=quad.at[quarter], dst_ref=quad.at[quarter],
            send_sem=q_ss.at[d], recv_sem=q_rs.at[d], device_id=(g, to * 2 + half), device_id_type=MESH,
        )

    for d in range(1, 4):
        q_copy(d).start()

    @pl.loop(1, 16)
    def _(r):
        c_copy(r).wait_recv()

    total = c_recv[0]
    for n in range(1, 16):
        total = total + c_recv[n]
    turned = pltpu.roll(total, 64, 1)
    both = [jnp.where(low64, total, turned), jnp.where(low64, turned, total)]
    r_id = iota((32, 128), 0)
    ia_label = occ_label(4 * g + r_id % 4) ^ vir_label(8 * s + r_id // 4)
    for part in range(4):
        c_full[part] = jnp.where(ia_label == jb_label[part], both[part // 2], f32(0.0))
    for i in range(4):
        for part in range(4):
            cyc_out[i, :, 128 * part : 128 * part + 128] = c_full[part, pl.ds(i, 8, stride=4), :]

    for d in range(1, 4):
        q_copy(d).wait_recv()

    b_label = vir_label(zero + z // 4) ^ vir_label(32 * (s % 8) + iota((32, 128), 0))
    full = quad[...].reshape(32, 256)
    for part in range(2):
        cols = slice(128 * part, 128 * part + 128)
        lad_out[:, cols] = jnp.where(ij_label[part] == b_label, full[:, cols], f32(0.0))

    for move in moves:
        move.wait_send()
    for d in range(1, 4):
        q_copy(d).wait_send()

    for n in range(4):
        y_copy(n).wait_send()

    @pl.loop(1, 16)
    def _(r):
        a_copy(r).wait_send()
        c_copy(r).wait_send()
        z_arrival(r).wait_send()


def folded_path(tiles, amplitudes, ladder_ints, cycle_ints, occ_irrep, vir_irrep):
    f32, bf16 = jnp.float32, jnp.bfloat16
    vmem = pltpu.VMEM
    dma = pltpu.SemaphoreType.DMA
    ladder, cycle, longest = pl.pallas_call(
        functools.partial(folded_kernel, tiles),
        out_shape=(
            jax.ShapeDtypeStruct((32, 256), f32),
            jax.ShapeDtypeStruct((4, 8, 512), f32),
            jax.ShapeDtypeStruct((1, 1), jnp.int32),
        ),
        in_specs=[pl.BlockSpec(memory_space=pl.ANY)] * 5,
        out_specs=[pl.BlockSpec(memory_space=pltpu.VMEM)] * 2 + [pl.BlockSpec(memory_space=pltpu.SMEM)],
        scratch_shapes=[
            vmem((1, 64), jnp.int32), vmem((1, 256), jnp.int32),
            vmem((256, 2048), f32), vmem((64, 2048), f32), vmem((1024, 512), f32),
            vmem((256, 128 * tiles), f32), vmem((256, 128 * tiles), bf16), vmem((256, 128 * tiles), bf16),
            vmem((16, tiles, 16, 128), f32), vmem((tiles, 256, 128), f32),
            vmem((256, 512), bf16), vmem((256, 512), bf16), vmem((16, 64, 128 * tiles), f32),
            vmem((2, 4, 32, 256), f32), vmem((4, 32, 256), f32), vmem((16, 8, 256), f32), vmem((16, 8, 256), f32),
            vmem((4, 8, 256), f32), vmem((512, 256), bf16), vmem((512, 256), bf16),
            vmem((512, 128), f32), vmem((16, 1, 32, 128), f32), vmem((16, 32, 128), f32), vmem((4, 32, 128), f32),
            dma((5,)), dma((17,)), dma((17,)), dma((16,)), dma((16,)), dma((4,)), dma((4,)),
            dma((16,)), dma((16,)), dma((4,)), dma((4,)), dma((16,)), dma((16,)),
            pltpu.SemaphoreType.REGULAR, pltpu.SemaphoreType.REGULAR,
        ],
        compiler_params=pltpu.CompilerParams(
            collective_id=0, has_side_effects=True, vmem_limit_bytes=62 * 1024 * 1024
        ),
        cost_estimate=pl.CostEstimate(flops=400_000_000, bytes_accessed=5_000_000, transcendentals=0),
    )(occ_irrep.reshape(1, -1), vir_irrep.reshape(1, -1), amplitudes, ladder_ints.T, cycle_ints)
    return ladder.T, cycle, longest[0, 0]


def per_device(amplitudes, ladder_ints, cycle_ints, occ_irrep, vir_irrep):
    ladder, cycle, longest = folded_path(TILES, amplitudes, ladder_ints, cycle_ints, occ_irrep, vir_irrep)
    return lax.cond(
        longest <= 16 * TILES,
        lambda: (ladder, cycle),
        lambda: dense_path(amplitudes, ladder_ints, cycle_ints, occ_irrep, vir_irrep),
    )


def solution(mesh):
    return jax.shard_map(
        per_device,
        mesh=mesh,
        in_specs=(P("grp", "slab"), P("slab", "grp"), P("grp", None), P(), P()),
        out_specs=(P("grp", "slab"), P("grp", "slab", None)),
        check_vma=False,
    )
```

```python
import functools

import jax
import jax.numpy as jnp
from jax import lax
from jax.experimental import pallas as pl
from jax.experimental.pallas import tpu as pltpu
from jax.sharding import PartitionSpec as P

TILES = 3
IRREPS = 8
MESH = pl.DeviceIdType.MESH


def allowed_mask(lab_i, lab_j, lab_a, lab_b):
    left = jnp.bitwise_xor(lab_i, lab_j)
    right = jnp.bitwise_xor(lab_a, lab_b)
    return left == right


def gather_cols(block):
    groups = lax.axis_size("grp")
    copies = jnp.broadcast_to(block[None], (groups,) + block.shape)
    parts = lax.all_to_all(copies, "grp", split_axis=0, concat_axis=0, tiled=True)
    return jnp.moveaxis(parts, 0, 1).reshape(block.shape[0], groups * block.shape[1])


def sum_parts(partial, axis, dim):
    count = lax.axis_size(axis)
    shape = partial.shape
    split = partial.reshape(shape[:dim] + (count, shape[dim] // count) + shape[dim + 1 :])
    parts = lax.all_to_all(split, axis, split_axis=dim, concat_axis=dim, tiled=True)
    return jnp.sum(parts, axis=dim)


def dense_path(amplitudes, ladder_ints, cycle_ints, occ_irrep, vir_irrep):
    groups = lax.axis_size("grp")
    slabs = lax.axis_size("slab")
    grp_index = lax.axis_index("grp")
    slab_index = lax.axis_index("slab")
    occ_count = occ_irrep.shape[0]
    vir_count = vir_irrep.shape[0]
    occ_local = amplitudes.shape[0] // occ_count
    vir_local = amplitudes.shape[1] // vir_count
    window = ladder_ints.shape[1] * groups
    ladder_cols = window // slabs
    a_count = window // vir_count
    partial_sum = jnp.dot(
        amplitudes,
        gather_cols(ladder_ints),
        precision=lax.Precision.HIGHEST,
        preferred_element_type=jnp.float32,
    )
    ladder = sum_parts(partial_sum, "slab", 1)
    occ_mine = lax.dynamic_slice_in_dim(occ_irrep, grp_index * occ_local, occ_local, 0)
    row_i = jnp.repeat(occ_mine, occ_count)
    row_j = jnp.tile(occ_irrep, occ_local)
    col_a = lax.dynamic_slice_in_dim(
        jnp.repeat(vir_irrep[:a_count], vir_count), slab_index * ladder_cols, ladder_cols, 0
    )
    col_b = lax.dynamic_slice_in_dim(
        jnp.tile(vir_irrep, a_count), slab_index * ladder_cols, ladder_cols, 0
    )
    ladder_keep = allowed_mask(row_i[:, None], row_j[:, None], col_a[None, :], col_b[None, :])
    ladder_term = jnp.where(ladder_keep, ladder, jnp.float32(0.0))
    blocks = amplitudes.reshape(occ_local, occ_count, vir_local, vir_count)
    k_local = cycle_ints.shape[0] // vir_count
    cycle_cols = cycle_ints.shape[1]
    cycle_table = cycle_ints.reshape(k_local, vir_count, cycle_cols)
    regrouped = lax.all_to_all(blocks, "grp", split_axis=1, concat_axis=0, tiled=True)
    partial_cycle = jnp.einsum(
        "ikac,kcw->iaw", regrouped, cycle_table, precision=lax.Precision.HIGHEST
    )
    cycle = sum_parts(partial_cycle, "grp", 0)
    j_count = cycle_cols // vir_count
    vir_mine = lax.dynamic_slice_in_dim(vir_irrep, slab_index * vir_local, vir_local, 0)
    col_j = jnp.repeat(occ_irrep[:j_count], vir_count)
    col_jb = jnp.tile(vir_irrep, j_count)
    cycle_keep = allowed_mask(
        occ_mine[:, None, None],
        col_j[None, None, :],
        vir_mine[None, :, None],
        col_jb[None, None, :],
    )
    cycle_term = jnp.where(cycle_keep, cycle, jnp.float32(0.0))
    return (ladder_term, cycle_term)


def folded_kernel(
    tiles,
    occ_hbm, vir_hbm, amp_hbm, lad_hbm, cyc_hbm, lad_out, cyc_out, run_out,
    occ_v, vir_v, amp, lad, cyc, amp_fold, amp_hi, amp_lo, a2a_send, a2a_recv, cyc_hi, cyc_lo, gath,
    zed, y_recv, z_send, z_recv, quad, lhs_hi, lhs_lo, c_part, c_send, c_recv, c_full,
    load_sem, g_ss, g_rs, a_ss, a_rs, y_ss, y_rs, z_ss, z_rs, q_ss, q_rs, c_ss, c_rs, here_sem, meet_sem,
):
    f32, i32, bf16 = jnp.float32, jnp.int32, jnp.bfloat16
    g, s = lax.axis_index("grp"), lax.axis_index("slab")
    core, x, y = g % 2, (g // 2) % 4, g // 8
    z, half = s // 2, s % 2

    load_l = pltpu.make_async_copy(lad_hbm, lad, load_sem.at[0])
    load_a = pltpu.make_async_copy(amp_hbm, amp, load_sem.at[1])
    load_w = pltpu.make_async_copy(cyc_hbm, cyc, load_sem.at[2])
    load_o = pltpu.make_async_copy(occ_hbm, occ_v, load_sem.at[3])
    load_v = pltpu.make_async_copy(vir_hbm, vir_v, load_sem.at[4])
    load_l.start()
    load_o.start()
    load_v.start()
    load_a.start()

    barrier = pltpu.get_barrier_semaphore()

    @pl.loop(1, 16)
    def _(r):
        to = (g + r) % 16

        @pl.when(to != 0)
        def _():
            pl.semaphore_signal(barrier, inc=1, device_id=(to, s), device_id_type=MESH)

    def iota(shape, dim):
        return lax.broadcasted_iota(i32, shape, dim)

    def split(value):
        high = value.astype(bf16)
        return high, (value - high.astype(f32)).astype(bf16)

    low64 = iota((1, 128), 1) < 64
    lane = iota((1, 128), 1)

    def pack_pair(first, second):
        keep = jnp.where(low64, first, second)
        move = jnp.where(low64, second, first)
        return keep + pltpu.roll(move, 64, 1)

    def spread(rows):
        turned = [row if n == 0 else pltpu.roll(row, 16 * n, 1) for n, row in enumerate(rows)]
        for bit in (1, 2, 4):
            here = (lane // 16) // bit % 2 == 1
            turned = [jnp.where(here, turned[(n + bit) % 8], turned[n]) for n in range(8)]
        return [turned[0]] + [pltpu.roll(turned[8 - p], 128 - 16 * p, 1) for p in range(1, 8)]

    def fold(src, rows):
        sums = [None] * tiles
        for part in range(2):
            runs = spread([src[rows, 256 * n + 128 * part : 256 * n + 128 * part + 128] for n in range(8)])
            for p in range(8):
                u = (8 * part + p) % tiles
                sums[u] = runs[p] if sums[u] is None else sums[u] + runs[p]
        return sums

    def regroup(src, dst, blocks):
        low4 = iota((8, 1), 0) < 4

        @pl.loop(0, 8)
        def _(q):
            for n in range(0, blocks, 2):
                for c in range(src.shape[1] // 128):
                    cols = slice(128 * c, 128 * c + 128)
                    one = src[pl.ds(pl.multiple_of(64 * n + 8 * q, 8), 8), cols]
                    two = src[pl.ds(pl.multiple_of(64 * n + 64 + 8 * q, 8), 8), cols]
                    dst[2 * q, c, 4 * n : 4 * n + 8, :] = jnp.where(low4, one, pltpu.roll(two, 4, 0))
                    dst[2 * q + 1, c, 4 * n : 4 * n + 8, :] = jnp.where(low4, pltpu.roll(one, 4, 0), two)

    load_l.wait()

    @pl.loop(0, 4)
    def _(r):
        rows = pl.ds(pl.multiple_of(16 * r, 16), 16)
        for u, folded in enumerate(fold(lad, rows)):
            gath[g, rows, 128 * u : 128 * u + 128] = folded

    @pl.when(g != 0)
    def _():
        pl.semaphore_wait(barrier, 15)

    @pl.when(g == 1)
    def _():
        pl.semaphore_signal(here_sem, inc=1, device_id=(0, s), device_id_type=MESH)

    @pl.when(g == 0)
    def _():
        pl.semaphore_wait(here_sem, 1)

        @pl.loop(1, 32)
        def _(r):
            pl.semaphore_signal(barrier, inc=1, device_id=(0, (s + r) % 32), device_id_type=MESH)

    def meet_slabs():
        @pl.when(g == 0)
        def _():
            pl.semaphore_wait(barrier, 31)

            @pl.loop(1, 16)
            def _(r):
                pl.semaphore_signal(meet_sem, inc=1, device_id=(r, s), device_id_type=MESH)

        @pl.when(g != 0)
        def _():
            pl.semaphore_wait(meet_sem, 1)

    def dev(y_, x_, core_):
        return (y_ * 4 + x_ % 4) * 2 + core_

    turn = 1 - 2 * (x % 2)
    sib, y_dev = dev(y, x, 1 - core), dev(1 - y, x, core)
    mate, other = dev(y, x + 4 + turn, core), dev(y, x + 4 - turn, core)
    y_mate, y_other = dev(1 - y, x + 4 + turn, core), dev(1 - y, x + 4 - turn, core)
    across, y_across = dev(y, x + 2, core), dev(1 - y, x + 2, core)

    def g_copy(k, slot, to, rows=None):
        ref = gath.at[slot] if rows is None else gath.at[slot, rows]
        return pltpu.make_async_remote_copy(
            src_ref=ref, dst_ref=ref, send_sem=g_ss.at[k], recv_sem=g_rs.at[k],
            device_id=(to, s), device_id_type=MESH,
        )

    lower, upper = pl.ds(0, 32), pl.ds(32, 32)
    moves = [
        g_copy(0, g, y_dev), g_copy(1, g, mate), g_copy(2, g, other), g_copy(3, g, sib),
        g_copy(4, y_dev, mate), g_copy(5, y_dev, other), g_copy(6, y_dev, sib),
        g_copy(7, mate, other, lower), g_copy(8, other, mate, upper),
        g_copy(9, y_mate, other, lower), g_copy(10, y_other, mate, upper),
        g_copy(11, mate, sib), g_copy(12, other, sib), g_copy(13, y_mate, sib), g_copy(14, y_other, sib),
        g_copy(15, across, sib), g_copy(16, y_across, sib),
    ]

    def go(*numbers):
        for k in numbers:
            moves[k].start()

    def got(*numbers):
        for k in numbers:
            moves[k].wait_recv()

    go(0, 1, 2, 3)

    load_a.wait()
    load_w.start()

    @pl.loop(0, 16)
    def _(r):
        rows = pl.ds(pl.multiple_of(16 * r, 16), 16)
        for u, folded in enumerate(fold(amp, rows)):
            cols = slice(128 * u, 128 * u + 128)
            amp_fold[rows, cols] = folded
            amp_hi[rows, cols], amp_lo[rows, cols] = split(folded)

    got(0)
    go(4, 5, 6)
    got(1)
    go(7, 11)
    got(2)
    go(8, 12)

    regroup(amp_fold, a2a_send, 4)
    mine16 = pl.ds(pl.multiple_of(16 * g, 16), 16)

    def a_copy(r):
        to = (g + r) % 16
        return pltpu.make_async_remote_copy(
            src_ref=a2a_send.at[to], dst_ref=a2a_recv.at[:, mine16],
            send_sem=a_ss.at[r], recv_sem=a_rs.at[r], device_id=(to, s), device_id_type=MESH,
        )

    load_o.wait()
    load_v.wait()

    def run_starts(ref):
        return [
            jnp.sum(jnp.where(ref[...] < v, 1.0, 0.0), axis=1, keepdims=True).astype(i32) for v in range(1, IRREPS)
        ]

    occ_starts, vir_starts = run_starts(occ_v), run_starts(vir_v)

    starts = [0] + vir_starts + [vir_v.shape[1]]
    longest = starts[1]
    for v in range(1, IRREPS):
        longest = jnp.maximum(longest, starts[v + 1] - starts[v])
    run_out[0, 0] = jnp.max(longest)

    def label(index, starts):
        total = jnp.where(index >= starts[0], 1, 0)
        for start in starts[1:]:
            total = total + jnp.where(index >= start, 1, 0)
        return total

    def occ_label(index):
        return label(index, occ_starts)

    def vir_label(index):
        return label(index, vir_starts)

    zero = jnp.zeros((1, 128), i32)

    def pair_label(part):
        return occ_label(4 * g + 2 * part + lane // 64) ^ occ_label(lane % 64)

    ij_label = [pair_label(part) for part in range(2)]
    row_label = [vir_label(iota((64, 128), 0) + 64 * m) for m in range(4)]

    def dot(first, second, dims):
        return lax.dot_general(first, second, (dims, ((), ())), preferred_element_type=f32)

    def dot3(a_hi, a_lo, b_hi, b_lo, dims):
        return dot(a_hi, b_hi, dims) + (dot(a_hi, b_lo, dims) + dot(a_lo, b_hi, dims))

    order = [2 * y + x // 2, 2 * (1 - y) + x // 2, 2 * y + 1 - x // 2, 2 * (1 - y) + 1 - x // 2]

    def y_copy(n):
        return pltpu.make_async_remote_copy(
            src_ref=zed.at[1 - half, order[n]], dst_ref=y_recv.at[order[n]],
            send_sem=y_ss.at[n], recv_sem=y_rs.at[n],
            device_id=(g, z * 2 + (1 - half)), device_id_type=MESH,
        )

    def z_copy(to):
        r = (to - z + 16) % 16
        return pltpu.make_async_remote_copy(
            src_ref=z_send.at[to], dst_ref=z_recv.at[z],
            send_sem=z_ss.at[r], recv_sem=z_rs.at[r], device_id=(g, to * 2 + half), device_id_type=MESH,
        )

    def ladder_product(n):
        a = order[n]
        hi, lo = split(gath[pl.ds(4 * a, 4)].reshape(256, 128 * tiles))
        product = dot3(hi, lo, amp_hi[...], amp_lo[...], ((1,), (1,)))
        a_label = vir_label(zero + a)
        for part in range(2):
            cols = slice(128 * part, 128 * part + 128)
            want = ij_label[part] ^ a_label
            total = jnp.where(row_label[0] == want, product[0:64, cols], f32(0.0))
            for m in range(1, 4):
                total = total + jnp.where(row_label[m] == want, product[64 * m : 64 * m + 64, cols], f32(0.0))
            zed[0, a, :, cols] = total[0:32]
            zed[1, a, :, cols] = total[32:64]
        y_copy(n).start()

    def ladder_sums(n):
        a = order[n]
        y_copy(n).wait_recv()
        total = zed[half, a] + y_recv[a]
        for q in range(4):
            z_send[4 * a + q] = total[8 * q : 8 * q + 8]
            to = 4 * a + q

            @pl.when(to != z)
            def _():
                z_copy(to).start()

    got(3, 11)
    meet_slabs()
    ladder_product(0)
    got(4)
    go(9, 13)
    got(5)
    go(10, 14)

    load_w.wait()

    @pl.loop(0, 4)
    def _(k):
        for u in range(tiles):
            part = cyc[pl.ds(pl.multiple_of(256 * k + 16 * u, 16), 16), :]
            for e in range(u + tiles, 16, tiles):
                part = part + cyc[pl.ds(pl.multiple_of(256 * k + 16 * e, 16), 16), :]
            rows = pl.ds(pl.multiple_of(16 * (tiles * k + u), 16), 16)
            cyc_hi[rows, :], cyc_lo[rows, :] = split(part)

    if tiles < 4:
        cyc_hi[64 * tiles : 256, :] = jnp.zeros((256 - 64 * tiles, 512), bf16)
        cyc_lo[64 * tiles : 256, :] = jnp.zeros((256 - 64 * tiles, 512), bf16)

    got(7, 8)
    go(15)
    got(6, 13)
    ladder_product(1)
    got(9, 10)
    go(16)

    @pl.loop(1, 16)
    def _(r):
        a_copy(r).start()

    a2a_recv[:, mine16, :] = a2a_send[g]

    ladder_sums(0)
    got(12, 15)
    ladder_product(2)
    ladder_sums(1)
    got(14, 16)
    ladder_product(3)
    ladder_sums(2)
    ladder_sums(3)
    z_recv[z] = z_send[z]

    @pl.loop(1, 16)
    def _(r):
        a_copy(r).wait_recv()

    for r in range(4):
        for w in range(2):
            pieces = []
            for q in range(8 * w, 8 * w + 8):
                k, u = q // tiles, q % tiles
                if k < 4:
                    pieces.append(a2a_recv[u, pl.ds(64 * r + k, 16, stride=4), :])
                else:
                    pieces.append(jnp.zeros((16, 128), f32))
            cols = slice(128 * w, 128 * w + 128)
            for a, value in enumerate(spread(pieces)):
                at = slice(64 * a + 16 * r, 64 * a + 16 * r + 16)
                lhs_hi[at, cols], lhs_lo[at, cols] = split(value)

    jb_label = [
        occ_label(zero + part // 2) ^ vir_label(lane + 128 * (part % 2)) for part in range(4)
    ]

    @pl.loop(0, 2)
    def _(h):
        rows = pl.ds(pl.multiple_of(256 * h, 256), 256)
        r_id = iota((256, 128), 0)
        ia_label = occ_label(r_id % 64) ^ vir_label(8 * s + 4 * h + r_id // 64)
        folds = []
        for j in range(2):
            cols = slice(256 * j, 256 * j + 256)
            product = dot3(lhs_hi[rows, :], lhs_lo[rows, :], cyc_hi[:, cols], cyc_lo[:, cols], ((1,), (0,)))
            kept = [
                jnp.where(ia_label == jb_label[2 * j + part], product[:, 128 * part : 128 * part + 128], f32(0.0))
                for part in range(2)
            ]
            folds.append(kept[0] + kept[1])
        c_part[rows, :] = pack_pair(folds[0], folds[1])

    regroup(c_part, c_send, 8)

    def c_copy(r):
        to = (g + r) % 16
        return pltpu.make_async_remote_copy(
            src_ref=c_send.at[to, 0], dst_ref=c_recv.at[g],
            send_sem=c_ss.at[r], recv_sem=c_rs.at[r], device_id=(to, s), device_id_type=MESH,
        )

    @pl.loop(1, 16)
    def _(r):
        c_copy(r).start()

    c_recv[g] = c_send[g, 0]

    def z_arrival(r):
        return pltpu.make_async_remote_copy(
            src_ref=z_send.at[z], dst_ref=z_recv.at[z], send_sem=z_ss.at[r], recv_sem=z_rs.at[r],
            device_id=(g, ((z + r) % 16) * 2 + half), device_id_type=MESH,
        )

    @pl.loop(1, 16)
    def _(r):
        z_arrival(r).wait_recv()

    total = z_recv[0]
    for n in range(1, 16):
        total = total + z_recv[n]
    quarter = z % 4
    quad[quarter] = total

    def q_copy(d):
        to = 4 * (z // 4) + (z + d) % 4
        return pltpu.make_async_remote_copy(
            src_ref=quad.at[quarter], dst_ref=quad.at[quarter],
            send_sem=q_ss.at[d], recv_sem=q_rs.at[d], device_id=(g, to * 2 + half), device_id_type=MESH,
        )

    for d in range(1, 4):
        q_copy(d).start()

    @pl.loop(1, 16)
    def _(r):
        c_copy(r).wait_recv()

    total = c_recv[0]
    for n in range(1, 16):
        total = total + c_recv[n]
    turned = pltpu.roll(total, 64, 1)
    both = [jnp.where(low64, total, turned), jnp.where(low64, turned, total)]
    r_id = iota((32, 128), 0)
    ia_label = occ_label(4 * g + r_id % 4) ^ vir_label(8 * s + r_id // 4)
    for part in range(4):
        c_full[part] = jnp.where(ia_label == jb_label[part], both[part // 2], f32(0.0))
    for i in range(4):
        for part in range(4):
            cyc_out[i, :, 128 * part : 128 * part + 128] = c_full[part, pl.ds(i, 8, stride=4), :]

    for d in range(1, 4):
        q_copy(d).wait_recv()

    b_label = vir_label(zero + z // 4) ^ vir_label(32 * (s % 8) + iota((32, 128), 0))
    full = quad[...].reshape(32, 256)
    for part in range(2):
        cols = slice(128 * part, 128 * part + 128)
        lad_out[:, cols] = jnp.where(ij_label[part] == b_label, full[:, cols], f32(0.0))

    for move in moves:
        move.wait_send()
    for d in range(1, 4):
        q_copy(d).wait_send()

    for n in range(4):
        y_copy(n).wait_send()

    @pl.loop(1, 16)
    def _(r):
        a_copy(r).wait_send()
        c_copy(r).wait_send()
        z_arrival(r).wait_send()


def folded_path(tiles, amplitudes, ladder_ints, cycle_ints, occ_irrep, vir_irrep):
    f32, bf16 = jnp.float32, jnp.bfloat16
    vmem = pltpu.VMEM
    dma = pltpu.SemaphoreType.DMA
    ladder, cycle, longest = pl.pallas_call(
        functools.partial(folded_kernel, tiles),
        out_shape=(
            jax.ShapeDtypeStruct((32, 256), f32),
            jax.ShapeDtypeStruct((4, 8, 512), f32),
            jax.ShapeDtypeStruct((1, 1), jnp.int32),
        ),
        in_specs=[pl.BlockSpec(memory_space=pl.ANY)] * 5,
        out_specs=[pl.BlockSpec(memory_space=pltpu.VMEM)] * 2 + [pl.BlockSpec(memory_space=pltpu.SMEM)],
        scratch_shapes=[
            vmem((1, 64), jnp.int32), vmem((1, 256), jnp.int32),
            vmem((256, 2048), f32), vmem((64, 2048), f32), vmem((1024, 512), f32),
            vmem((256, 128 * tiles), f32), vmem((256, 128 * tiles), bf16), vmem((256, 128 * tiles), bf16),
            vmem((16, tiles, 16, 128), f32), vmem((tiles, 256, 128), f32),
            vmem((256, 512), bf16), vmem((256, 512), bf16), vmem((16, 64, 128 * tiles), f32),
            vmem((2, 4, 32, 256), f32), vmem((4, 32, 256), f32), vmem((16, 8, 256), f32), vmem((16, 8, 256), f32),
            vmem((4, 8, 256), f32), vmem((512, 256), bf16), vmem((512, 256), bf16),
            vmem((512, 128), f32), vmem((16, 1, 32, 128), f32), vmem((16, 32, 128), f32), vmem((4, 32, 128), f32),
            dma((5,)), dma((17,)), dma((17,)), dma((16,)), dma((16,)), dma((4,)), dma((4,)),
            dma((16,)), dma((16,)), dma((4,)), dma((4,)), dma((16,)), dma((16,)),
            pltpu.SemaphoreType.REGULAR, pltpu.SemaphoreType.REGULAR,
        ],
        compiler_params=pltpu.CompilerParams(
            collective_id=0, has_side_effects=True, vmem_limit_bytes=62 * 1024 * 1024
        ),
        cost_estimate=pl.CostEstimate(flops=400_000_000, bytes_accessed=5_000_000, transcendentals=0),
    )(occ_irrep.reshape(1, -1), vir_irrep.reshape(1, -1), amplitudes, ladder_ints.T, cycle_ints)
    return ladder.T, cycle, longest[0, 0]


def per_device(amplitudes, ladder_ints, cycle_ints, occ_irrep, vir_irrep):
    ladder, cycle, longest = folded_path(TILES, amplitudes, ladder_ints, cycle_ints, occ_irrep, vir_irrep)
    return lax.cond(
        longest <= 16 * TILES,
        lambda: (ladder, cycle),
        lambda: dense_path(amplitudes, ladder_ints, cycle_ints, occ_irrep, vir_irrep),
    )


def solution(mesh):
    return jax.shard_map(
        per_device,
        mesh=mesh,
        in_specs=(P("grp", "slab"), P("slab", "grp"), P("grp", None), P(), P()),
        out_specs=(P("grp", "slab"), P("grp", "slab", None)),
        check_vma=False,
    )
```
